128 devices in a mesh: tile: 16 (over x, y), lev: 8 (over z, core).
Axes of the slice: x: 4, y: 4, z: 4, core: 2. Of those that a mesh axis runs over, the one named last changes fastest.
Arguments:
- anomalies: bfloat16 [64, 32768, 256], P('lev', 'tile'), may hold values from -12 to 12
- mean_state: float32 [64, 32768], P('lev', 'tile'), may hold values from -6 to 6
- obs_op: bfloat16 [65536, 4096], P(('tile', 'lev')), may hold values from -0.005859375 to 0.005859375
- innovations: float32 [4194304], P(('tile', 'lev')), may hold values from -24 to 24
- obs_rinv: float32 [4194304], P(('tile', 'lev')), may hold values from 0.25 to 4
- obs_cols: int32 [524288], P(('tile', 'lev')), may hold values from 0 to 2431, as said below
- send_cols: int32 [16, 384], P('tile'), may hold values from 0 to 2047
- obs_count: int32 [128], P(('tile', 'lev')), may hold values from 1 to 512, 32768 in all
Outputs:
- analysis: bfloat16 [64, 32768, 256], P('lev', 'tile')
The draws below stay inside these ranges and needn't reach their ends.
Inputs may be any that keep to these rules, and one draw needn't show every extreme that they name: `obs_cols`: an entry below 2048 names the block's own tile's column of that number; an entry 2048 + p * 24 + s names the column in slot s of tile p's send list for this tile. `send_cols`: row p, entries t * 24 to t * 24 + 23 are the own columns tile p sends to tile t. `obs_count`: blocks of a device beyond its count are padding.
All inputs are finite; a program needn't handle non-finite values.
Results may differ from the reference program's by a relative error of at most 0.0083.
Values may be sent and summed in bfloat16 or wider, within the bound.
No kernel may reach another device: no remote copies, remote signals or barrier semaphores. Data moves between devices by JAX's collectives and lax.ppermute only.
A program may use at most 192 MiB of HBM per device.

```python
import math
from functools import partial
import jax
import jax.numpy as jnp
import numpy as np
from jax import lax

K = 256
OBS_B = 64
SUPP = 8
LEV_DEV = 8
COLS_DEV = 2048
NB = 512
CAP = 24
NLEV = 64
NCOL = 32768
NB_ALL = 65536
SLOTS = 384
N_TILE = 16
N_LEV = 8
DEVICES = 128


def draw_anomalies(key, part):
    key = jax.random.fold_in(key, 11)
    subkeys = jax.random.split(key, 4)
    full_shape = (NLEV, NCOL, K)
    member_scale = jnp.exp(jax.random.uniform(subkeys[0], (K,), jnp.float32, math.log(0.3), math.log(3.0)))
    white_noise = jax.random.normal(subkeys[1], full_shape, jnp.float32)
    fields = jax.random.normal(subkeys[2], (4, NLEV, NCOL, 1), jnp.float32)
    loadings = 0.6 * jax.random.normal(subkeys[3], (4, K), jnp.float32)
    combined = white_noise * member_scale
    for mode_index in range(4):
        combined = combined + fields[mode_index] * loadings[mode_index]
    return jnp.clip(combined, -12.0, 12.0).astype(jnp.bfloat16)


def draw_innovations(key, part):
    key = jax.random.fold_in(key, 37)
    count_all = NB_ALL * OBS_B
    owner = (jnp.arange(count_all, dtype=jnp.int32) // (NB * OBS_B)).astype(jnp.float32)
    position = owner / max(DEVICES - 1, 1)
    noise = jax.random.normal(key, (count_all,), jnp.float32)
    growth = math.log(5.0)
    return jnp.clip(noise * jnp.exp(growth * position), -24.0, 24.0)


def draw_obs_cols(key, part):
    key = jax.random.fold_in(key, 23)
    subkeys = jax.random.split(key, 3)
    count_all = NB_ALL * SUPP
    own_index = jax.random.randint(subkeys[0], (count_all,), 0, COLS_DEV)
    face_index = COLS_DEV + jax.random.randint(subkeys[1], (count_all,), 0, SLOTS)
    choose_face = jax.random.randint(subkeys[2], (count_all,), 0, 2)
    picked = jnp.where(choose_face == 1, face_index, own_index)
    picked = picked.at[0].set(0).at[count_all - 1].set(COLS_DEV + SLOTS - 1)
    return picked.astype(jnp.int32)


def touch_ends(drawn, key, smallest, high):
    extent = drawn.shape
    spot = [jax.random.randint(jax.random.fold_in(key, axis), (), 0, extent[axis]) for axis in range(len(extent))]
    drawn = drawn.at[tuple(spot)].set(smallest)
    longest = extent.index(max(extent))
    spot[longest] = (spot[longest] + 1) % extent[longest]
    return drawn.at[tuple(spot)].set(high)


def block_levels(own_key, extent, cuts, smallest, top_value):
    def one(dim, blocks):
        steps = jax.random.uniform(jax.random.fold_in(jax.random.fold_in(own_key, 6), dim), (blocks,), jnp.float32, smallest / len(cuts), top_value / len(cuts))
        return jnp.repeat(jnp.exp(steps), extent[dim] // blocks).reshape((-1,) + (1,) * (len(extent) - dim - 1))

    factor_of = one(*cuts[0])
    for cut in cuts[1:]:
        factor_of = factor_of * one(*cut)
    return factor_of


def split_up(number_of, total, most, skew):
    loads = [(1 << 20) // math.isqrt(standing ** skew) + 1 for standing in range(2, number_of + 1)]
    spare, holding = total - most - (number_of - 1), [1] * (number_of - 1)
    while spare > 0:
        free = [i for i in range(number_of - 1) if holding[i] < most]
        whole, budget = sum([loads[i] for i in free]), spare
        for i in free:
            extra = min(most - holding[i], max(1, budget * loads[i] // whole), spare)
            holding[i] = holding[i] + extra
            spare = spare - extra
    return np.array([most] + holding)


def uneven(own_key, amount, total, most, lean):
    if amount == 2:
        one = jax.random.randint(own_key, (), max(1, total - most), min(most, total - 1) + 1)
        return jnp.stack([one, total - one])
    lengths = jnp.asarray(split_up(amount, total, most, lean), jnp.int32)
    couples = (amount - 1) // 2
    donor, sink = lengths[1:1 + 2 * couples:2], lengths[2:2 + 2 * couples:2]
    room = jnp.minimum(donor - 1, most - sink)
    passed = jax.random.randint(jax.random.fold_in(own_key, 1), (couples,), 0, 1 << 20) % (room + 1)
    lengths = lengths.at[1:1 + 2 * couples:2].set(donor - passed).at[2:2 + 2 * couples:2].set(sink + passed)
    return lengths[jax.random.permutation(jax.random.fold_in(own_key, 2), amount)]


def normal_values(stream_key, shape, width, bound, cuts=(), kind=jnp.bfloat16):
    drawn = width * jax.random.normal(stream_key, shape, jnp.float32)
    if cuts:
        drawn = drawn * block_levels(stream_key, shape, cuts, -0.22, 0.18)
    return jnp.clip(drawn, -bound, bound).astype(kind)


def setup_inputs(seed: int = 0) -> dict:
    splits = jax.random.split(jax.random.key(seed), 9)
    return {
        "anomalies": draw_anomalies(jax.random.fold_in(splits[8], 71), 0),
        "mean_state": normal_values(splits[1], (NLEV, NCOL), 1.0, 6.0, ((0, 8), (1, 16)), jnp.float32),
        "obs_op": normal_values(splits[2], (NB_ALL, OBS_B * SUPP * LEV_DEV), (SUPP * LEV_DEV * NB * OBS_B * DEVICES // K) ** -0.5, 0.005859375, ((0, 128),)),
        "innovations": draw_innovations(jax.random.fold_in(splits[8], 71), 0),
        "obs_rinv": jnp.clip(jnp.exp(math.log(4.0) - 2.7725887 * jax.random.uniform(splits[4], (NB_ALL * OBS_B,), jnp.float32) ** block_levels(splits[4], (NB_ALL * OBS_B,), ((0, 128),), -0.2, 0.2)), 0.25, 4.0),
        "obs_cols": draw_obs_cols(jax.random.fold_in(splits[8], 71), 0),
        "send_cols": touch_ends(jax.random.randint(splits[6], (N_TILE, SLOTS), 0, COLS_DEV), jax.random.fold_in(splits[6], 1), 0, COLS_DEV - 1).astype(jnp.int32),
        "obs_count": uneven(splits[7], DEVICES, NB * DEVICES // 2, NB, 2).astype(jnp.int32),
    }


HIGH = lax.Precision.HIGHEST

def square_root(spread):
    values, vectors = jnp.linalg.eigh(spread)
    return jnp.dot(vectors * jnp.sqrt(values)[None, :], vectors.T, precision=HIGH)

def transform_weights(gram_sym, projection, numerator, obs_total, members):
    rho_value = numerator / obs_total
    identity = jnp.eye(members, dtype=jnp.float32)
    system = (members - 1.0) / rho_value * identity + gram_sym
    factor = jnp.linalg.cholesky(system)
    inverse = jax.scipy.linalg.cho_solve((factor, True), identity)
    mean_weights = jnp.dot(inverse, projection, precision=HIGH)
    spread = (members - 1.0) * inverse
    spread = 0.5 * (spread + spread.T)
    root = square_root(spread)
    return (root + mean_weights[:, None]).astype(jnp.bfloat16)

def device_terms(anomalies, obs_op, innovations, obs_rinv, obs_cols, send_cols, obs_count, device):
    tile_index = device // N_LEV
    group_index = device % N_LEV
    own_columns = tile_index * COLS_DEV + jnp.arange(COLS_DEV, dtype=jnp.int32)
    listed = lax.dynamic_slice_in_dim(send_cols, (tile_index * CAP).astype(jnp.int32), CAP, 1)
    remote = (jnp.arange(N_TILE, dtype=jnp.int32)[:, None] * COLS_DEV + listed).reshape(-1)
    ext_cols = jnp.concatenate([own_columns, remote]).astype(jnp.int32)
    first_block = (device * NB).astype(jnp.int32)
    block_ops = lax.dynamic_slice_in_dim(obs_op, first_block, NB, 0).astype(jnp.float32)
    block_ops = block_ops.reshape(NB, OBS_B, SUPP, LEV_DEV)
    references = lax.dynamic_slice_in_dim(obs_cols, first_block * SUPP, NB * SUPP, 0)
    global_cols = ext_cols[references]
    lev_ids = (group_index * LEV_DEV + jnp.arange(LEV_DEV, dtype=jnp.int32)).astype(jnp.int32)
    support = anomalies[lev_ids[:, None], global_cols[None, :], :].astype(jnp.float32)
    support = support.reshape(LEV_DEV, NB, SUPP, K)
    images = jnp.einsum('boql,lbqk->bok', block_ops, support, precision=HIGH)
    rinv_blocks = lax.dynamic_slice_in_dim(obs_rinv, first_block * OBS_B, NB * OBS_B, 0).reshape(NB, OBS_B)
    innov_blocks = lax.dynamic_slice_in_dim(innovations, first_block * OBS_B, NB * OBS_B, 0).reshape(NB, OBS_B)
    live_mask = jnp.arange(NB, dtype=jnp.int32)[:, None] < obs_count[device]
    obs_weight = jnp.where(live_mask, jnp.sqrt(rinv_blocks), 0.0)
    scaled = (obs_weight[:, :, None] * images).astype(jnp.bfloat16).reshape(NB * OBS_B, K)
    scaled_wide = scaled.astype(jnp.float32)
    gram = jnp.dot(scaled_wide.T, scaled_wide, precision=HIGH)
    projection = jnp.dot((obs_weight * innov_blocks).reshape(-1), scaled_wide, precision=HIGH)
    numerator = jnp.sum(jnp.where(live_mask, rinv_blocks * innov_blocks * innov_blocks, 0.0))
    return (gram, projection, numerator)

def reference(anomalies, mean_state, obs_op, innovations, obs_rinv, obs_cols, send_cols, obs_count):
    terms = lax.map(partial(device_terms, anomalies, obs_op, innovations, obs_rinv, obs_cols, send_cols, obs_count), jnp.arange(DEVICES, dtype=jnp.int32))
    gram = lax.optimization_barrier(jnp.sum(terms[0], axis=0))
    gram_sym = 0.5 * (gram + gram.T)
    projection = lax.optimization_barrier(jnp.sum(terms[1], axis=0))
    numerator = jnp.sum(terms[2])
    obs_total = jnp.sum(obs_count).astype(jnp.float32) * OBS_B
    transform = transform_weights(gram_sym, projection, numerator, obs_total, K)
    transform_wide = transform.astype(jnp.float32)

    def apply_level(level_pair):
        level_anoms, level_mean = level_pair
        updated = jnp.dot(level_anoms.astype(jnp.float32), transform_wide, precision=HIGH)
        return (level_mean[:, None] + updated).astype(jnp.bfloat16)
    return lax.map(apply_level, (anomalies, mean_state))
```

```python
import functools

import jax
import jax.numpy as jnp
from jax import lax
from jax.experimental import pallas as pl
from jax.experimental.pallas import tpu as pltpu
from jax.sharding import PartitionSpec as P

F32 = jnp.float32
BF16 = jnp.bfloat16
AXES = ("tile", "lev")
VMEM_BYTES = 60 << 20
GROUP = 16
CHUNK = 64
PACK = 104


def split3(value):
    high = value.astype(BF16)
    rest = value - high.astype(F32)
    middle = rest.astype(BF16)
    low = (rest - middle.astype(F32)).astype(BF16)
    return high, middle, low


def send_kernel(send_ref, anom_ref, out_ref, level_ref, wide_ref, sems):
    lev_dev, col_dev, members = anom_ref.shape
    slots = send_ref.shape[1]
    copies = [
        pltpu.make_async_copy(anom_ref.at[v], level_ref.at[v], sems.at[v]) for v in range(lev_dev)
    ]
    for copy in copies:
        copy.start()
    listed = jnp.broadcast_to(send_ref[...].astype(F32), (8, slots)).T[:, 0:1]
    lanes = lax.broadcasted_iota(jnp.int32, (slots, col_dev), 1).astype(F32)
    chosen = jnp.where(lanes == listed, 1.0, 0.0).astype(BF16)
    for v in range(lev_dev):
        copies[v].wait()
        rows = jnp.dot(chosen, level_ref[v], preferred_element_type=F32)
        for h in range(members // 128):
            wide_ref.at[h][pl.ds(v, slots, stride=lev_dev), :] = rows[:, h * 128 : (h + 1) * 128]
    for h in range(members // 128):
        half = wide_ref[h].reshape(slots, lev_dev, 128)
        out_ref[:, :, h * 128 : (h + 1) * 128] = half.astype(BF16)


def gather_sent(send_cols, anomalies):
    lev_dev, col_dev, members = anomalies.shape
    slots = send_cols.shape[1]
    return pl.pallas_call(
        send_kernel,
        in_specs=[pl.BlockSpec(memory_space=pltpu.VMEM), pl.BlockSpec(memory_space=pl.ANY)],
        out_specs=pl.BlockSpec(memory_space=pltpu.VMEM),
        out_shape=jax.ShapeDtypeStruct((slots, lev_dev, members), BF16),
        scratch_shapes=[
            pltpu.VMEM((lev_dev, col_dev, members), BF16),
            pltpu.VMEM((members // 128, slots * lev_dev, 128), F32),
            pltpu.SemaphoreType.DMA((lev_dev,)),
        ],
        compiler_params=pltpu.CompilerParams(vmem_limit_bytes=VMEM_BYTES),
        name="gather_sent",
    )(send_cols, anomalies)


def prepare_kernel(count_ref, op_ref, rinv_ref, innov_ref, pair_ref, sums_ref, wide_ref):
    blocks, width = op_ref.shape
    per_block = rinv_ref.shape[1]
    points = width // per_block
    tiles = width // 128
    count = count_ref[0]
    spread_row = lax.broadcasted_iota(jnp.int32, (per_block, width), 0)
    spread_lane = lax.broadcasted_iota(jnp.int32, (per_block, width), 1)
    expand = jnp.where(spread_lane // points == spread_row, 1.0, 0.0).astype(BF16)
    live = lax.broadcasted_iota(jnp.int32, (blocks, per_block), 0) < count
    innov = innov_ref[...]
    squares = jnp.where(live, rinv_ref[...] * innov * innov, 0.0)
    numerator = jnp.sum(squares, axis=(0, 1), keepdims=True)
    total = jnp.full((1, 1), count * per_block, jnp.int32).astype(F32)
    lane = lax.broadcasted_iota(jnp.int32, (8, 256), 1)
    sums_ref[...] = jnp.where(lane == 0, numerator, jnp.where(lane == 1, total, 0.0))
    low_half = lax.broadcasted_iota(jnp.int32, (1, 1, 128), 2) < points

    def chunk(step, carried):
        start = pl.multiple_of(step * CHUNK, CHUNK)
        alive = start + lax.broadcasted_iota(jnp.int32, (CHUNK, per_block), 0) < count
        weight = jnp.where(alive, jnp.sqrt(rinv_ref[pl.ds(start, CHUNK), :]), 0.0)
        parts = split3(weight)
        wide = jnp.dot(parts[0], expand, preferred_element_type=F32)
        wide = wide + jnp.dot(parts[1], expand, preferred_element_type=F32)
        wide = wide + jnp.dot(parts[2], expand, preferred_element_type=F32)
        weighted = op_ref[pl.ds(start, CHUNK), :].astype(F32) * wide
        for r in range(tiles):
            wide_ref[pl.ds(r, CHUNK, stride=tiles), :] = weighted[:, r * 128 : (r + 1) * 128]
        rows = wide_ref[...].reshape(CHUNK // 2, 2, tiles, 128)
        first, second = rows[:, 0], rows[:, 1]
        first_turned = pltpu.roll(first.reshape(-1, 128), 64, 1).reshape(first.shape)
        second_turned = pltpu.roll(second.reshape(-1, 128), 64, 1).reshape(second.shape)
        pieces = [
            jnp.where(low_half, first, 0.0),
            jnp.where(low_half, first_turned, 0.0),
            jnp.where(low_half, 0.0, second_turned),
            jnp.where(low_half, 0.0, second),
        ]
        out = pl.multiple_of(step * (CHUNK // 2), CHUNK // 2)
        pair_ref[pl.ds(out, CHUNK // 2)] = jnp.concatenate(pieces, axis=1).astype(BF16)
        return carried

    lax.fori_loop(0, blocks // CHUNK, chunk, 0)


def prepare(obs_count, obs_op, rinv_blocks, innov_blocks):
    blocks = obs_op.shape[0]
    vmem = pl.BlockSpec(memory_space=pltpu.VMEM)
    return pl.pallas_call(
        prepare_kernel,
        in_specs=[pl.BlockSpec(memory_space=pltpu.SMEM), vmem, vmem, vmem],
        out_specs=[vmem, vmem],
        out_shape=[
            jax.ShapeDtypeStruct((blocks // 2, 128, 128), BF16),
            jax.ShapeDtypeStruct((8, 256), F32),
        ],
        scratch_shapes=[pltpu.VMEM((CHUNK * 32, 128), F32)],
        compiler_params=pltpu.CompilerParams(vmem_limit_bytes=VMEM_BYTES),
        name="prepare_operators",
    )(obs_count, obs_op, rinv_blocks, innov_blocks)


def gram_kernel(
    cols_ref, count_ref, core_ref, own_ref, remote_ref, pair_ref, innov_ref, sums_ref,
    keep_ref, give_ref, table, pairs, support, scaled, total, sems,
):
    own_cols = own_ref.shape[0]
    n_pairs = pair_ref.shape[0]
    chunk_pairs = CHUNK // 2
    chunks = n_pairs // chunk_pairs
    own = pltpu.make_async_copy(own_ref, table.at[pl.ds(0, own_cols)], sems.at[chunks])
    remote = pltpu.make_async_copy(
        remote_ref, table.at[pl.ds(own_cols, remote_ref.shape[0])], sems.at[chunks + 1]
    )
    own.start()
    remote.start()
    fetches = []
    for k in range(chunks):
        part = pl.ds(k * chunk_pairs, chunk_pairs)
        fetches.append(pltpu.make_async_copy(pair_ref.at[part], pairs.at[part], sems.at[k]))
        fetches[k].start()
    total[...] = jnp.zeros_like(total)
    groups = (count_ref[0] + GROUP - 1) // GROUP
    own.wait()
    remote.wait()

    def step(g, carried):
        for i in range(GROUP * 8):
            support[i] = table[cols_ref[g * (GROUP * 8) + i]]
        for j in range(GROUP // 2):
            points = support[j * 16 : (j + 1) * 16].reshape(128, 256)
            images = jnp.dot(pairs[g * (GROUP // 2) + j], points, preferred_element_type=F32)
            scaled[j * 128 : (j + 1) * 128, :] = images.astype(BF16)
        rows = scaled[...]
        parts = split3(innov_ref[pl.ds(g, 1), :])
        row_index = lax.broadcasted_iota(jnp.int32, (16, GROUP * 64), 0)
        extra = jnp.where(row_index == 0, parts[0].astype(F32), 0.0)
        extra = jnp.where(row_index == 1, parts[1].astype(F32), extra)
        extra = jnp.where(row_index == 2, parts[2].astype(F32), extra).astype(BF16)
        left = jnp.concatenate([rows.T, extra], axis=0)
        total[...] += jnp.dot(left, rows, preferred_element_type=F32)
        return carried

    per_chunk = CHUNK // GROUP
    for k in range(chunks):
        fetches[k].wait()
        last = jnp.minimum(groups, (k + 1) * per_chunk)
        lax.fori_loop(k * per_chunk, jnp.maximum(last, k * per_chunk), step, 0)

    projection = total[256:257, :] + total[257:258, :] + total[258:259, :]
    row = lax.broadcasted_iota(jnp.int32, (8, 256), 0)
    ending = jnp.where(row == 0, projection, jnp.where(row == 1, sums_ref[...], 0.0))
    zeros = jnp.zeros((8, 256), F32)
    first = total[0:PACK, :]
    corner = jnp.concatenate([total[128:192, 128:256], total[192:256, 128:256]], axis=1)
    second = jnp.concatenate([total[PACK:128, :], corner, ending, zeros], axis=0)
    core = core_ref[0]

    @pl.when(core == 0)
    def _():
        keep_ref[...] = first
        give_ref[...] = second

    @pl.when(core != 0)
    def _():
        keep_ref[...] = second
        give_ref[...] = first


def gram_sums(obs_cols, obs_count, core, own, remote, pairs, innov_rows, sums):
    vmem = pl.BlockSpec(memory_space=pltpu.VMEM)
    smem = pl.BlockSpec(memory_space=pltpu.SMEM)
    anywhere = pl.BlockSpec(memory_space=pl.ANY)
    half = jax.ShapeDtypeStruct((PACK, 256), F32)
    chunks = pairs.shape[0] // (CHUNK // 2)
    return pl.pallas_call(
        gram_kernel,
        in_specs=[smem, smem, smem, anywhere, anywhere, anywhere, vmem, vmem],
        out_specs=[vmem, vmem],
        out_shape=[half, half],
        scratch_shapes=[
            pltpu.VMEM((own.shape[0] + remote.shape[0],) + own.shape[1:], BF16),
            pltpu.VMEM(pairs.shape, BF16),
            pltpu.VMEM((GROUP * 8, 8, 256), BF16),
            pltpu.VMEM((GROUP * 64, 256), BF16),
            pltpu.VMEM((272, 256), F32),
            pltpu.SemaphoreType.DMA((chunks + 2,)),
        ],
        compiler_params=pltpu.CompilerParams(vmem_limit_bytes=VMEM_BYTES),
        name="gram_sums",
    )(obs_cols, obs_count, core, own, remote, pairs, innov_rows, sums)


def dot3(left, right):
    left_high = left.astype(BF16)
    left_low = (left - left_high.astype(F32)).astype(BF16)
    right_high = right.astype(BF16)
    right_low = (right - right_high.astype(F32)).astype(BF16)
    return jnp.dot(
        jnp.concatenate([left_high, left_high, left_low], axis=1),
        jnp.concatenate([right_high, right_low, right_high], axis=0),
        preferred_element_type=F32,
    )


def apply_kernel(
    core_ref, mine_ref, other_ref, mean_ref, anom_ref, out_ref,
    levels, results, approx_ref, inverse_ref, in_sems, out_sems,
):
    lev_dev = anom_ref.shape[0]
    members = anom_ref.shape[2]
    loads = [
        pltpu.make_async_copy(anom_ref.at[v], levels.at[v], in_sems.at[v]) for v in range(lev_dev)
    ]
    for load in loads:
        load.start()
    core = core_ref[0]
    mine, other = mine_ref[...], other_ref[...]
    first = jnp.where(core == 0, mine, other)
    second = jnp.where(core == 0, other, mine)
    upper = jnp.concatenate([first, second[: 128 - PACK]], axis=0)
    packed = second[128 - PACK : 192 - PACK]
    corner = jnp.concatenate([packed[:, :128], packed[:, 128:]], axis=0)
    projection = second[192 - PACK : 193 - PACK]
    sums = second[193 - PACK : 194 - PACK]
    side = upper[:, 128:]
    gram = jnp.concatenate([upper, jnp.concatenate([side.T, corner], axis=1)], axis=0)
    gram = 0.5 * (gram + gram.T)

    numerator, obs_total = sums[:, 0:1], sums[:, 1:2]
    shift = (members - 1.0) * obs_total / numerator
    rows = lax.broadcasted_iota(jnp.int32, (members, members), 0)
    lanes = lax.broadcasted_iota(jnp.int32, (members, members), 1)
    identity = jnp.where(rows == lanes, 1.0, 0.0)
    system = gram + shift * identity
    norm = jnp.sqrt(jnp.sum(system * system, axis=(0, 1), keepdims=True))
    approx_ref[...] = system / norm
    inverse_ref[...] = identity
    lowest = jnp.minimum(jnp.sqrt(shift / norm), 1.0)[0, 0]

    def advance(scale):
        approx, inverse = approx_ref[...], inverse_ref[...]
        middle = (1.5 * scale) * identity - (0.5 * scale * scale * scale) * dot3(inverse, approx)
        approx_ref[...] = dot3(approx, middle)
        inverse_ref[...] = dot3(middle, inverse)

    def more(carried):
        turn, low = carried
        return jnp.logical_and(turn < 60, low < 0.999)

    def turn_once(carried):
        turn, low = carried
        x = jnp.maximum(low, 0.02)
        scale = 1.7323 + x * (-0.88804 + x * (-0.071549 + x * (0.385863 - 0.15965 * x)))
        scale = jnp.maximum(scale, 1.0)
        advance(scale)
        at_low = 0.5 * scale * low * (3.0 - scale * scale * low * low)
        at_one = 0.5 * scale * (3.0 - scale * scale)
        return turn + 1, jnp.minimum(at_low, at_one)

    lax.while_loop(more, turn_once, (jnp.int32(0), lowest))
    advance(1.0)
    inverse = inverse_ref[...]
    line = jnp.broadcast_to(projection, (128, members)).T
    weights = dot3(inverse, dot3(inverse, line)) / norm
    root = (jnp.sqrt((members - 1.0) / norm)) * inverse
    transform = (root + jnp.concatenate([weights, weights], axis=1)).astype(BF16)

    means = mean_ref[...].T
    stores = []
    for v in range(lev_dev):
        loads[v].wait()
        updated = jnp.dot(levels[v], transform, preferred_element_type=F32)
        results[v] = (means[:, v : v + 1] + updated).astype(BF16)
        stores.append(pltpu.make_async_copy(results.at[v], out_ref.at[v], out_sems.at[v]))
        stores[v].start()
    for store in stores:
        store.wait()


def solve_and_apply(core, mine, other, mean_state, anomalies):
    vmem = pl.BlockSpec(memory_space=pltpu.VMEM)
    anywhere = pl.BlockSpec(memory_space=pl.ANY)
    lev_dev, _, members = anomalies.shape
    return pl.pallas_call(
        apply_kernel,
        in_specs=[pl.BlockSpec(memory_space=pltpu.SMEM), vmem, vmem, vmem, anywhere],
        out_specs=anywhere,
        out_shape=jax.ShapeDtypeStruct(anomalies.shape, BF16),
        scratch_shapes=[
            pltpu.VMEM(anomalies.shape, BF16),
            pltpu.VMEM(anomalies.shape, BF16),
            pltpu.VMEM((members, members), F32),
            pltpu.VMEM((members, members), F32),
            pltpu.SemaphoreType.DMA((lev_dev,)),
            pltpu.SemaphoreType.DMA((lev_dev,)),
        ],
        compiler_params=pltpu.CompilerParams(vmem_limit_bytes=VMEM_BYTES),
        name="solve_and_apply",
    )(core, mine, other, mean_state, anomalies)


def turns(devices, stride, distance):
    pairs = []
    for device in range(devices):
        place = (device // stride) % 4
        pairs.append((device, device + ((place + distance) % 4 - place) * stride))
    return pairs


def sum_over(value, devices, stride):
    arrived = [lax.ppermute(value, AXES, turns(devices, stride, d)) for d in (2, 1, 3)]
    return (value + arrived[0]) + (arrived[1] + arrived[2])


def per_device(
    devices, anomalies, mean_state, obs_op, innovations, obs_rinv, obs_cols, send_cols, obs_count
):
    blocks = obs_op.shape[0]
    per_block = innovations.shape[0] // blocks
    core = (lax.axis_index("lev") % 2).astype(jnp.int32).reshape(1)
    outgoing = gather_sent(send_cols, anomalies)
    remote = lax.all_to_all(outgoing, "tile", split_axis=0, concat_axis=0, tiled=True)

    own = jnp.transpose(anomalies, (1, 0, 2))
    rinv_blocks = obs_rinv.reshape(blocks, per_block)
    innov_blocks = innovations.reshape(blocks, per_block)
    pairs, sums = prepare(obs_count, obs_op, rinv_blocks, innov_blocks)
    weighted = jnp.sqrt(rinv_blocks) * innov_blocks
    weighted = jnp.where(jnp.arange(blocks)[:, None] < obs_count[0], weighted, 0.0)
    weighted = weighted.reshape(blocks, per_block // 2, 2).swapaxes(1, 2)
    innov_rows = weighted.reshape(blocks // GROUP, GROUP * per_block)

    keep, give = gram_sums(obs_cols, obs_count, core, own, remote, pairs, innov_rows, sums)
    value = keep + lax.ppermute(give, AXES, [(d, d ^ 1) for d in range(devices)])
    for stride in (2, 8, 32):
        value = sum_over(value, devices, stride)
    other = lax.ppermute(value, AXES, [(d, d ^ 1) for d in range(devices)])
    return solve_and_apply(core, value, other, mean_state, anomalies)


def solution(mesh):
    return jax.shard_map(
        functools.partial(per_device, mesh.size),
        mesh=mesh,
        in_specs=(
            P("lev", "tile", None),
            P("lev", "tile"),
            P(("tile", "lev"), None),
            P(("tile", "lev")),
            P(("tile", "lev")),
            P(("tile", "lev")),
            P("tile", None),
            P(("tile", "lev")),
        ),
        out_specs=P("lev", "tile", None),
        check_vma=False,
    )
```

```python
import functools

import jax
import jax.numpy as jnp
from jax import lax
from jax.experimental import pallas as pl
from jax.experimental.pallas import tpu as pltpu
from jax.sharding import PartitionSpec as P

F32 = jnp.float32
BF16 = jnp.bfloat16
AXES = ("tile", "lev")
GROUP = 64
CHUNK = 64
PACK = 104


def split3(value):
    high = value.astype(BF16)
    rest = value - high.astype(F32)
    middle = rest.astype(BF16)
    low = (rest - middle.astype(F32)).astype(BF16)
    return high, middle, low


def send_kernel(send_ref, anom_ref, out_ref, levels, wide, sems):
    lev_dev, col_dev, members = anom_ref.shape
    slots = out_ref.shape[0]
    copies = [
        pltpu.make_async_copy(anom_ref.at[v], levels.at[v], sems.at[v]) for v in range(lev_dev)
    ]
    for copy in copies:
        copy.start()
    rows = 512

    for v in range(lev_dev):
        copies[v].wait()

        def spread(step, carried, v=v):
            start = pl.multiple_of(step * rows, rows)
            part = levels[v, pl.ds(start, rows), :].astype(F32)
            for h in range(members // 128):
                place = pl.ds(start * lev_dev + v, rows, stride=lev_dev)
                wide.at[h][place, :] = part[:, h * 128 : (h + 1) * 128]
            return carried

        lax.fori_loop(0, col_dev // rows, spread, 0)

    def pick(step, carried):
        for i in range(32):
            slot = step * 32 + i
            place = pl.ds(pl.multiple_of(send_ref[0, slot] * lev_dev, lev_dev), lev_dev)
            for h in range(members // 128):
                out_ref[slot, :, h * 128 : (h + 1) * 128] = wide[h, place, :].astype(BF16)
        return carried

    lax.fori_loop(0, slots // 32, pick, 0)


def gather_sent(send_cols, anomalies):
    lev_dev, col_dev, members = anomalies.shape
    slots = send_cols.shape[1]
    return pl.pallas_call(
        send_kernel,
        in_specs=[pl.BlockSpec(memory_space=pltpu.SMEM), pl.BlockSpec(memory_space=pl.ANY)],
        out_specs=pl.BlockSpec(memory_space=pltpu.VMEM),
        out_shape=jax.ShapeDtypeStruct((slots, lev_dev, members), BF16),
        scratch_shapes=[
            pltpu.VMEM((lev_dev, col_dev, members), BF16),
            pltpu.VMEM((members // 128, col_dev * lev_dev, 128), F32),
            pltpu.SemaphoreType.DMA((lev_dev,)),
        ],
        compiler_params=pltpu.CompilerParams(vmem_limit_bytes=60 << 20),
        name="gather_sent",
    )(send_cols, anomalies)


def prepare_kernel(
    count_ref, op_ref, rinv_ref, innov_ref, pair_ref, sums_ref,
    ops, expand, wide, folded, built, in_sems, out_sems,
):
    blocks, width = op_ref.shape
    per_block = rinv_ref.shape[1]
    points = width // per_block
    tiles = width // 128
    count = count_ref[0]
    steps = blocks // CHUNK
    loads = []
    for k in range(steps):
        part = pl.ds(k * CHUNK, CHUNK)
        loads.append(pltpu.make_async_copy(op_ref.at[part], ops.at[part], in_sems.at[k]))
        loads[k].start()
    spread_row = lax.broadcasted_iota(jnp.int32, (2 * per_block, width), 0) % per_block
    spread_lane = lax.broadcasted_iota(jnp.int32, (2 * per_block, width), 1) // points
    expand[...] = jnp.where(spread_lane == spread_row, 1.0, 0.0).astype(BF16)
    live = lax.broadcasted_iota(jnp.int32, (blocks, per_block), 0) < count
    innov = innov_ref[...]
    squares = jnp.where(live, rinv_ref[...] * innov * innov, 0.0)
    numerator = jnp.sum(squares, axis=(0, 1), keepdims=True)
    total = jnp.full((1, 1), count * per_block, jnp.int32).astype(F32)
    lane = lax.broadcasted_iota(jnp.int32, (8, 256), 1)
    sums_ref[...] = jnp.where(lane == 0, numerator, jnp.where(lane == 1, total, 0.0))
    low_half = lax.broadcasted_iota(jnp.int32, (1, 128), 1) < points
    extra_row = lax.broadcasted_iota(jnp.int32, (CHUNK // 2, 16, 128), 1)

    def store(k):
        part = pl.ds(k * (CHUNK // 2), CHUNK // 2)
        return pltpu.make_async_copy(built.at[k % 2], pair_ref.at[part], out_sems.at[k % 2])

    for k in range(steps):
        start = k * CHUNK
        alive = start + lax.broadcasted_iota(jnp.int32, (CHUNK, per_block), 0) < count
        rinv = jnp.where(alive, rinv_ref[start : start + CHUNK, :], 0.0)
        factors = jnp.concatenate([jnp.sqrt(rinv), rinv * innov_ref[start : start + CHUNK, :]], 0)
        high, middle, _ = split3(factors)
        both = jnp.concatenate([high, middle], axis=1)
        loads[k].wait()
        column = jnp.zeros((CHUNK, 128), F32)
        for t in range(tiles // 2):
            lanes = slice(t * 256, (t + 1) * 256)
            spread = jnp.dot(both, expand[:, lanes], preferred_element_type=F32)
            part = ops[start : start + CHUNK, lanes].astype(F32)
            weighted = part * spread[:CHUNK]
            pulled = part * spread[CHUNK:]
            column = column + (pulled[:, :128] + pulled[:, 128:])
            wide[pl.ds(2 * t, CHUNK, stride=tiles), :] = weighted[:, :128]
            wide[pl.ds(2 * t + 1, CHUNK, stride=tiles), :] = weighted[:, 128:]
        folded[...] = column + pltpu.roll(column, points, 1)
        if k >= 2:
            store(k - 2).wait()
        slot = built.at[k % 2]
        column = jnp.where(
            low_half,
            folded[pl.ds(0, CHUNK // 2, stride=2), :],
            folded[pl.ds(1, CHUNK // 2, stride=2), :],
        )
        high, middle, low = [piece.astype(F32)[:, None, :] for piece in split3(column)]
        extra = jnp.where(extra_row == 2, low, 0.0)
        extra = jnp.where(extra_row == 1, middle, extra)
        slot[:, 128:144, :] = jnp.where(extra_row == 0, high, extra).astype(BF16)

        def pair_up(step, carried, slot=slot):
            for i in range(8):
                pair = step * 8 + i
                place = pl.multiple_of(pair * 2 * tiles, 2 * tiles)
                first = wide[pl.ds(place, tiles), :]
                second = wide[pl.ds(place + tiles, tiles), :]
                pieces = [
                    jnp.where(low_half, first, 0.0),
                    jnp.where(low_half, pltpu.roll(first, points, 1), 0.0),
                    jnp.where(low_half, 0.0, pltpu.roll(second, points, 1)),
                    jnp.where(low_half, 0.0, second),
                ]
                for q in range(4):
                    slot[pair, q * tiles : (q + 1) * tiles, :] = pieces[q].astype(BF16)
            return carried

        lax.fori_loop(0, CHUNK // 16, pair_up, 0)
        store(k).start()
    store(steps - 2).wait()
    store(steps - 1).wait()


def prepare(obs_count, obs_op, rinv_blocks, innov_blocks):
    blocks, width = obs_op.shape
    vmem = pl.BlockSpec(memory_space=pltpu.VMEM)
    anywhere = pl.BlockSpec(memory_space=pl.ANY)
    return pl.pallas_call(
        prepare_kernel,
        in_specs=[pl.BlockSpec(memory_space=pltpu.SMEM), anywhere, vmem, vmem],
        out_specs=[anywhere, vmem],
        out_shape=[
            jax.ShapeDtypeStruct((blocks // 2, 144, 128), BF16),
            jax.ShapeDtypeStruct((8, 256), F32),
        ],
        scratch_shapes=[
            pltpu.VMEM((blocks, width), BF16),
            pltpu.VMEM((128, width), BF16),
            pltpu.VMEM((CHUNK * width // 128, 128), F32),
            pltpu.VMEM((CHUNK, 128), F32),
            pltpu.VMEM((2, CHUNK // 2, 144, 128), BF16),
            pltpu.SemaphoreType.DMA((blocks // CHUNK,)),
            pltpu.SemaphoreType.DMA((2,)),
        ],
        compiler_params=pltpu.CompilerParams(vmem_limit_bytes=60 << 20),
        name="prepare_operators",
    )(obs_count, obs_op, rinv_blocks, innov_blocks)


def gram_kernel(
    cols_ref, count_ref, core_ref, own_ref, remote_ref, pair_ref, sums_ref,
    keep_ref, give_ref, table, pairs, support, scaled, total, pulled, sems,
):
    own_cols = own_ref.shape[0]
    n_pairs = pair_ref.shape[0]
    group_pairs = GROUP // 2
    most = n_pairs // group_pairs
    own = pltpu.make_async_copy(own_ref, table.at[pl.ds(0, own_cols)], sems.at[most])
    remote = pltpu.make_async_copy(
        remote_ref, table.at[pl.ds(own_cols, remote_ref.shape[0])], sems.at[most + 1]
    )
    own.start()
    remote.start()
    groups = (count_ref[0] + GROUP - 1) // GROUP

    def fetch(g):
        part = pl.ds(g * group_pairs, group_pairs)
        return pltpu.make_async_copy(pair_ref.at[part], pairs.at[part], sems.at[g])

    def begin(g, carried):
        fetch(g).start()
        return carried

    lax.fori_loop(0, groups, begin, 0)
    total[...] = jnp.zeros_like(total)
    pulled[...] = jnp.zeros_like(pulled)
    own.wait()
    remote.wait()

    def step(g, carried):
        fetch(g).wait()
        for i in range(GROUP * 8):
            support[i] = table[cols_ref[g * (GROUP * 8) + i]]
        extra = jnp.zeros((16, 256), F32)
        for j in range(group_pairs):
            points = support[j * 16 : (j + 1) * 16].reshape(128, 256)
            images = jnp.dot(pairs[g * group_pairs + j], points, preferred_element_type=F32)
            scaled[j * 128 : (j + 1) * 128, :] = images[:128].astype(BF16)
            extra = extra + images[128:]
        pulled[...] += extra
        rows = scaled[...]
        total[...] += lax.dot_general(
            rows, rows, (((0,), (0,)), ((), ())), preferred_element_type=F32
        )
        return carried

    lax.fori_loop(0, groups, step, 0)

    projection = pulled[0:1, :] + pulled[1:2, :] + pulled[2:3, :]
    row = lax.broadcasted_iota(jnp.int32, (8, 256), 0)
    ending = jnp.where(row == 0, projection, jnp.where(row == 1, sums_ref[...], 0.0))
    zeros = jnp.zeros((8, 256), F32)
    first = total[0:PACK, :]
    corner = jnp.concatenate([total[128:192, 128:256], total[192:256, 128:256]], axis=1)
    second = jnp.concatenate([total[PACK:128, :], corner, ending, zeros], axis=0)
    core = core_ref[0]

    @pl.when(core == 0)
    def _():
        keep_ref[...] = first
        give_ref[...] = second

    @pl.when(core != 0)
    def _():
        keep_ref[...] = second
        give_ref[...] = first


def gram_sums(obs_cols, obs_count, core, own, remote, pairs, sums):
    vmem = pl.BlockSpec(memory_space=pltpu.VMEM)
    smem = pl.BlockSpec(memory_space=pltpu.SMEM)
    anywhere = pl.BlockSpec(memory_space=pl.ANY)
    half = jax.ShapeDtypeStruct((PACK, 256), F32)
    most = pairs.shape[0] // (GROUP // 2)
    return pl.pallas_call(
        gram_kernel,
        in_specs=[smem, smem, smem, anywhere, anywhere, anywhere, vmem],
        out_specs=[vmem, vmem],
        out_shape=[half, half],
        scratch_shapes=[
            pltpu.VMEM((own.shape[0] + remote.shape[0],) + own.shape[1:], BF16),
            pltpu.VMEM(pairs.shape, BF16),
            pltpu.VMEM((GROUP * 8, 8, 256), BF16),
            pltpu.VMEM((GROUP * 64, 256), BF16),
            pltpu.VMEM((256, 256), F32),
            pltpu.VMEM((16, 256), F32),
            pltpu.SemaphoreType.DMA((most + 2,)),
        ],
        compiler_params=pltpu.CompilerParams(vmem_limit_bytes=56 << 20),
        name="gram_sums",
    )(obs_cols, obs_count, core, own, remote, pairs, sums)


def dot3(left, right):
    left_high = left.astype(BF16)
    left_low = (left - left_high.astype(F32)).astype(BF16)
    right_high = right.astype(BF16)
    right_low = (right - right_high.astype(F32)).astype(BF16)
    return jnp.dot(
        jnp.concatenate([left_high, left_high, left_low], axis=1),
        jnp.concatenate([right_high, right_low, right_high], axis=0),
        preferred_element_type=F32,
    )


def apply_kernel(
    core_ref, mine_ref, other_ref, mean_ref, anom_ref, out_ref,
    levels, results, approx_ref, inverse_ref, in_sems, out_sems,
):
    lev_dev = anom_ref.shape[0]
    members = anom_ref.shape[2]
    loads = [
        pltpu.make_async_copy(anom_ref.at[v], levels.at[v], in_sems.at[v]) for v in range(lev_dev)
    ]
    for load in loads:
        load.start()
    core = core_ref[0]
    mine, other = mine_ref[...], other_ref[...]
    first = jnp.where(core == 0, mine, other)
    second = jnp.where(core == 0, other, mine)
    upper = jnp.concatenate([first, second[: 128 - PACK]], axis=0)
    packed = second[128 - PACK : 192 - PACK]
    corner = jnp.concatenate([packed[:, :128], packed[:, 128:]], axis=0)
    projection = second[192 - PACK : 193 - PACK]
    sums = second[193 - PACK : 194 - PACK]
    side = upper[:, 128:]
    gram = jnp.concatenate([upper, jnp.concatenate([side.T, corner], axis=1)], axis=0)
    gram = 0.5 * (gram + gram.T)

    numerator, obs_total = sums[:, 0:1], sums[:, 1:2]
    shift = (members - 1.0) * obs_total / numerator
    rows = lax.broadcasted_iota(jnp.int32, (members, members), 0)
    lanes = lax.broadcasted_iota(jnp.int32, (members, members), 1)
    identity = jnp.where(rows == lanes, 1.0, 0.0)
    system = gram + shift * identity
    norm = jnp.sqrt(jnp.sum(system * system, axis=(0, 1), keepdims=True))
    approx_ref[...] = system / norm
    inverse_ref[...] = identity
    lowest = jnp.minimum(jnp.sqrt(shift / norm), 1.0)[0, 0]

    def advance(scale):
        approx, inverse = approx_ref[...], inverse_ref[...]
        middle = (1.5 * scale) * identity - (0.5 * scale * scale * scale) * dot3(inverse, approx)
        approx_ref[...] = dot3(approx, middle)
        inverse_ref[...] = dot3(middle, inverse)

    def more(carried):
        turn, low = carried
        return jnp.logical_and(turn < 60, low < 0.999)

    def turn_once(carried):
        turn, low = carried
        x = jnp.maximum(low, 0.02)
        scale = 1.7323 + x * (-0.88804 + x * (-0.071549 + x * (0.385863 - 0.15965 * x)))
        scale = jnp.maximum(scale, 1.0)
        advance(scale)
        at_low = 0.5 * scale * low * (3.0 - scale * scale * low * low)
        at_one = 0.5 * scale * (3.0 - scale * scale)
        return turn + 1, jnp.minimum(at_low, at_one)

    lax.while_loop(more, turn_once, (jnp.int32(0), lowest))
    advance(1.0)
    inverse = inverse_ref[...]
    line = jnp.broadcast_to(projection, (128, members)).T
    weights = dot3(inverse, dot3(inverse, line)) / norm
    root = (jnp.sqrt((members - 1.0) / norm)) * inverse
    transform = (root + jnp.concatenate([weights, weights], axis=1)).astype(BF16)

    means = mean_ref[...].T
    stores = []
    for v in range(lev_dev):
        loads[v].wait()
        updated = jnp.dot(levels[v], transform, preferred_element_type=F32)
        results[v] = (means[:, v : v + 1] + updated).astype(BF16)
        stores.append(pltpu.make_async_copy(results.at[v], out_ref.at[v], out_sems.at[v]))
        stores[v].start()
    for store in stores:
        store.wait()


def solve_and_apply(core, mine, other, mean_state, anomalies):
    vmem = pl.BlockSpec(memory_space=pltpu.VMEM)
    anywhere = pl.BlockSpec(memory_space=pl.ANY)
    lev_dev, _, members = anomalies.shape
    return pl.pallas_call(
        apply_kernel,
        in_specs=[pl.BlockSpec(memory_space=pltpu.SMEM), vmem, vmem, vmem, anywhere],
        out_specs=anywhere,
        out_shape=jax.ShapeDtypeStruct(anomalies.shape, BF16),
        scratch_shapes=[
            pltpu.VMEM(anomalies.shape, BF16),
            pltpu.VMEM(anomalies.shape, BF16),
            pltpu.VMEM((members, members), F32),
            pltpu.VMEM((members, members), F32),
            pltpu.SemaphoreType.DMA((lev_dev,)),
            pltpu.SemaphoreType.DMA((lev_dev,)),
        ],
        compiler_params=pltpu.CompilerParams(vmem_limit_bytes=58 << 20),
        name="solve_and_apply",
    )(core, mine, other, mean_state, anomalies)


def turns(devices, stride, distance):
    pairs = []
    for device in range(devices):
        place = (device // stride) % 4
        pairs.append((device, device + ((place + distance) % 4 - place) * stride))
    return pairs


def sum_over(value, devices, stride):
    arrived = [lax.ppermute(value, AXES, turns(devices, stride, d)) for d in (2, 1, 3)]
    return (value + arrived[0]) + (arrived[1] + arrived[2])


def per_device(
    devices, anomalies, mean_state, obs_op, innovations, obs_rinv, obs_cols, send_cols, obs_count
):
    blocks = obs_op.shape[0]
    per_block = innovations.shape[0] // blocks
    core = (lax.axis_index("lev") % 2).astype(jnp.int32).reshape(1)
    outgoing = gather_sent(send_cols, anomalies)
    remote = lax.all_to_all(outgoing, "tile", split_axis=0, concat_axis=0, tiled=True)

    own = jnp.transpose(anomalies, (1, 0, 2))
    rinv_blocks = obs_rinv.reshape(blocks, per_block)
    innov_blocks = innovations.reshape(blocks, per_block)
    pairs, sums = prepare(obs_count, obs_op, rinv_blocks, innov_blocks)
    keep, give = gram_sums(obs_cols, obs_count, core, own, remote, pairs, sums)
    value = keep + lax.ppermute(give, AXES, [(d, d ^ 1) for d in range(devices)])
    for stride in (2, 8, 32):
        value = sum_over(value, devices, stride)
    other = lax.ppermute(value, AXES, [(d, d ^ 1) for d in range(devices)])
    return solve_and_apply(core, value, other, mean_state, anomalies)


def solution(mesh):
    return jax.shard_map(
        functools.partial(per_device, mesh.size),
        mesh=mesh,
        in_specs=(
            P("lev", "tile", None),
            P("lev", "tile"),
            P(("tile", "lev"), None),
            P(("tile", "lev")),
            P(("tile", "lev")),
            P(("tile", "lev")),
            P("tile", None),
            P(("tile", "lev")),
        ),
        out_specs=P("lev", "tile", None),
        check_vma=False,
    )
```

```python
import functools

import jax
import jax.numpy as jnp
from jax import lax
from jax.experimental import pallas as pl
from jax.experimental.pallas import tpu as pltpu
from jax.sharding import PartitionSpec as P

F32 = jnp.float32
BF16 = jnp.bfloat16
AXES = ("tile", "lev")
GROUP = 128
CHUNK = 64
PACK = 104


def split3(value):
    high = value.astype(BF16)
    rest = value - high.astype(F32)
    middle = rest.astype(BF16)
    low = (rest - middle.astype(F32)).astype(BF16)
    return high, middle, low


def send_kernel(send_ref, anom_ref, out_ref, levels, wide, sems):
    lev_dev, col_dev, members = anom_ref.shape
    slots = out_ref.shape[0]
    copies = [
        pltpu.make_async_copy(anom_ref.at[v], levels.at[v], sems.at[v]) for v in range(lev_dev)
    ]
    for copy in copies:
        copy.start()
    rows = 512

    for v in range(lev_dev):
        copies[v].wait()

        def spread(step, carried, v=v):
            start = pl.multiple_of(step * rows, rows)
            part = levels[v, pl.ds(start, rows), :].astype(F32)
            for h in range(members // 128):
                place = pl.ds(start * lev_dev + v, rows, stride=lev_dev)
                wide.at[h][place, :] = part[:, h * 128 : (h + 1) * 128]
            return carried

        lax.fori_loop(0, col_dev // rows, spread, 0)

    def pick(step, carried):
        for i in range(32):
            slot = step * 32 + i
            place = pl.ds(pl.multiple_of(send_ref[0, slot] * lev_dev, lev_dev), lev_dev)
            for h in range(members // 128):
                out_ref[slot, :, h * 128 : (h + 1) * 128] = wide[h, place, :].astype(BF16)
        return carried

    lax.fori_loop(0, slots // 32, pick, 0)


def gather_sent(send_cols, anomalies):
    lev_dev, col_dev, members = anomalies.shape
    slots = send_cols.shape[1]
    return pl.pallas_call(
        send_kernel,
        in_specs=[pl.BlockSpec(memory_space=pltpu.SMEM), pl.BlockSpec(memory_space=pl.ANY)],
        out_specs=pl.BlockSpec(memory_space=pltpu.VMEM),
        out_shape=jax.ShapeDtypeStruct((slots, lev_dev, members), BF16),
        scratch_shapes=[
            pltpu.VMEM((lev_dev, col_dev, members), BF16),
            pltpu.VMEM((members // 128, col_dev * lev_dev, 128), F32),
            pltpu.SemaphoreType.DMA((lev_dev,)),
        ],
        compiler_params=pltpu.CompilerParams(vmem_limit_bytes=60 << 20),
        name="gather_sent",
    )(send_cols, anomalies)


def prepare_kernel(
    count_ref, op_ref, rinv_ref, innov_ref, anom_ref, pair_ref, sums_ref, own_ref,
    ops, levels, expand, wide, folded, built, turned, in_sems, anom_sems, out_sems, own_sems,
):
    blocks, width = op_ref.shape
    per_block = rinv_ref.shape[1]
    points = width // per_block
    tiles = width // 128
    count = count_ref[0]
    steps = blocks // CHUNK
    loads = []
    for k in range(steps):
        part = pl.ds(k * CHUNK, CHUNK)
        loads.append(pltpu.make_async_copy(op_ref.at[part], ops.at[part], in_sems.at[k]))
        loads[k].start()
    col_dev = anom_ref.shape[1]
    some = col_dev // steps
    reads = []
    for k in range(steps):
        part = pl.ds(k * some, some)
        reads.append(
            pltpu.make_async_copy(anom_ref.at[:, part], levels.at[:, part], anom_sems.at[k])
        )
        reads[k].start()
    spread_row = lax.broadcasted_iota(jnp.int32, (2 * per_block, 256), 0)
    spread_row = jnp.where(spread_row < per_block, spread_row, spread_row - per_block) * points
    ahead = lax.broadcasted_iota(jnp.int32, (2 * per_block, 256), 1) - spread_row
    for t in range(tiles // 2):
        inside = jnp.logical_and(ahead >= -t * 256, ahead < points - t * 256)
        expand[:, t * 256 : (t + 1) * 256] = jnp.where(inside, 1.0, 0.0).astype(BF16)
    live = lax.broadcasted_iota(jnp.int32, (blocks, per_block), 0) < count
    innov = innov_ref[...]
    squares = jnp.where(live, rinv_ref[...] * innov * innov, 0.0)
    numerator = jnp.sum(squares, axis=(0, 1), keepdims=True)
    total = jnp.full((1, 1), count * per_block, jnp.int32).astype(F32)
    lane = lax.broadcasted_iota(jnp.int32, (8, 256), 1)
    sums_ref[...] = jnp.where(lane == 0, numerator, jnp.where(lane == 1, total, 0.0))
    low_half = lax.broadcasted_iota(jnp.int32, (1, 128), 1) < points
    extra_row = lax.broadcasted_iota(jnp.int32, (CHUNK // 2, 16, 128), 1)

    def store(k):
        part = pl.ds(k * (CHUNK // 2), CHUNK // 2)
        return pltpu.make_async_copy(built.at[k % 2], pair_ref.at[part], out_sems.at[k % 2])

    def store_own(k):
        part = pl.ds(k * some, some)
        return pltpu.make_async_copy(turned.at[k % 2], own_ref.at[part], own_sems.at[k % 2])

    for k in range(steps):
        start = k * CHUNK
        alive = start + lax.broadcasted_iota(jnp.int32, (CHUNK, per_block), 0) < count
        rinv = jnp.where(alive, rinv_ref[start : start + CHUNK, :], 0.0)
        factors = jnp.concatenate([jnp.sqrt(rinv), rinv * innov_ref[start : start + CHUNK, :]], 0)
        high, middle, _ = split3(factors)
        both = jnp.concatenate([high, middle], axis=1)
        loads[k].wait()
        column = jnp.zeros((CHUNK, 128), F32)
        for t in range(tiles // 2):
            lanes = slice(t * 256, (t + 1) * 256)
            spread = jnp.dot(both, expand[:, lanes], preferred_element_type=F32)
            part = ops[start : start + CHUNK, lanes].astype(F32)
            weighted = part * spread[:CHUNK]
            pulled = part * spread[CHUNK:]
            column = column + (pulled[:, :128] + pulled[:, 128:])
            wide[pl.ds(2 * t, CHUNK, stride=tiles), :] = weighted[:, :128]
            wide[pl.ds(2 * t + 1, CHUNK, stride=tiles), :] = weighted[:, 128:]
        folded[...] = column + pltpu.roll(column, points, 1)
        if k >= 2:
            store(k - 2).wait()
        slot = built.at[k % 2]
        column = jnp.where(
            low_half,
            folded[pl.ds(0, CHUNK // 2, stride=2), :],
            folded[pl.ds(1, CHUNK // 2, stride=2), :],
        )
        high, middle, low = [piece.astype(F32)[:, None, :] for piece in split3(column)]
        extra = jnp.where(extra_row == 2, low, 0.0)
        extra = jnp.where(extra_row == 1, middle, extra)
        slot[:, 128:144, :] = jnp.where(extra_row == 0, high, extra).astype(BF16)

        def pair_up(step, carried, slot=slot):
            for i in range(CHUNK // 2):
                pair = step * (CHUNK // 2) + i
                place = pl.multiple_of(pair * 2 * tiles, 2 * tiles)
                first = wide[pl.ds(place, tiles), :]
                second = wide[pl.ds(place + tiles, tiles), :]
                pieces = [
                    jnp.where(low_half, first, 0.0),
                    jnp.where(low_half, pltpu.roll(first, points, 1), 0.0),
                    jnp.where(low_half, 0.0, pltpu.roll(second, points, 1)),
                    jnp.where(low_half, 0.0, second),
                ]
                for q in range(4):
                    slot[pair, q * tiles : (q + 1) * tiles, :] = pieces[q].astype(BF16)
            return carried

        lax.fori_loop(0, 1, pair_up, 0)
        store(k).start()
        reads[k].wait()
        if k >= 2:
            store_own(k - 2).wait()
        turned[k % 2] = jnp.swapaxes(levels[:, k * some : (k + 1) * some, :], 0, 1)
        store_own(k).start()
    store_own(steps - 2).wait()
    store_own(steps - 1).wait()
    store(steps - 2).wait()
    store(steps - 1).wait()


def prepare(obs_count, obs_op, rinv_blocks, innov_blocks, anomalies):
    blocks, width = obs_op.shape
    lev_dev, col_dev, members = anomalies.shape
    steps = blocks // CHUNK
    vmem = pl.BlockSpec(memory_space=pltpu.VMEM)
    anywhere = pl.BlockSpec(memory_space=pl.ANY)
    return pl.pallas_call(
        prepare_kernel,
        in_specs=[pl.BlockSpec(memory_space=pltpu.SMEM), anywhere, vmem, vmem, anywhere],
        out_specs=[anywhere, vmem, anywhere],
        out_shape=[
            jax.ShapeDtypeStruct((blocks // 2, 144, 128), BF16),
            jax.ShapeDtypeStruct((8, 256), F32),
            jax.ShapeDtypeStruct((col_dev, lev_dev, members), BF16),
        ],
        scratch_shapes=[
            pltpu.VMEM((blocks, width), BF16),
            pltpu.VMEM(anomalies.shape, BF16),
            pltpu.VMEM((128, width), BF16),
            pltpu.VMEM((CHUNK * width // 128, 128), F32),
            pltpu.VMEM((CHUNK, 128), F32),
            pltpu.VMEM((2, CHUNK // 2, 144, 128), BF16),
            pltpu.VMEM((2, col_dev // steps, lev_dev, members), BF16),
            pltpu.SemaphoreType.DMA((steps,)),
            pltpu.SemaphoreType.DMA((steps,)),
            pltpu.SemaphoreType.DMA((2,)),
            pltpu.SemaphoreType.DMA((2,)),
        ],
        compiler_params=pltpu.CompilerParams(vmem_limit_bytes=60 << 20),
        name="prepare_operators",
    )(obs_count, obs_op, rinv_blocks, innov_blocks, anomalies)


def gram_kernel(
    cols_ref, count_ref, core_ref, own_ref, remote_ref, pair_ref, sums_ref,
    keep_ref, give_ref, table, pairs, support_a, support_b, scaled_a, scaled_b, total, pulled, sems,
):
    own_cols = own_ref.shape[0]
    group_pairs = GROUP // 2
    own = pltpu.make_async_copy(own_ref, table.at[pl.ds(0, own_cols)], sems.at[2])
    remote = pltpu.make_async_copy(
        remote_ref, table.at[pl.ds(own_cols, remote_ref.shape[0])], sems.at[3]
    )
    own.start()
    remote.start()
    groups = (count_ref[0] + GROUP - 1) // GROUP

    def fetch(g):
        part = pl.ds(g * group_pairs, group_pairs)
        return pltpu.make_async_copy(pair_ref.at[part], pairs.at[g % 2], sems.at[g % 2])

    fetch(0).start()
    total[...] = jnp.zeros_like(total)
    pulled[...] = jnp.zeros_like(pulled)
    remote.wait()
    own.wait()

    half = GROUP // 2
    most_halves = cols_ref.shape[0] // (half * 8)

    def collect(h, support):
        place = jnp.minimum(h, most_halves - 1) * (half * 8)
        for i in range(half * 8):
            support[i] = table[cols_ref[place + i]]

    def add(operators, first, support, scaled):
        extra = jnp.zeros((16, 256), F32)
        for j in range(half // 2):
            points = support[j * 16 : (j + 1) * 16].reshape(128, 256)
            images = jnp.dot(operators[first + j], points, preferred_element_type=F32)
            scaled[j * 128 : (j + 1) * 128, :] = images[:128].astype(BF16)
            extra = extra + images[128:]
        pulled[...] += extra
        rows = scaled[...]
        total[...] += lax.dot_general(
            rows, rows, (((0,), (0,)), ((), ())), preferred_element_type=F32
        )

    def step(g, carried):
        fetch(g).wait()

        @pl.when(g + 1 < groups)
        def _():
            fetch(g + 1).start()

        operators = pairs.at[g % 2]
        collect(2 * g + 1, support_b)
        add(operators, 0, support_a, scaled_a)
        collect(2 * g + 2, support_a)
        add(operators, half // 2, support_b, scaled_b)
        return carried

    collect(0, support_a)
    lax.fori_loop(0, groups, step, 0)

    projection = pulled[0:1, :] + pulled[1:2, :] + pulled[2:3, :]
    row = lax.broadcasted_iota(jnp.int32, (8, 256), 0)
    ending = jnp.where(row == 0, projection, jnp.where(row == 1, sums_ref[...], 0.0))
    zeros = jnp.zeros((8, 256), F32)
    first = total[0:PACK, :]
    corner = jnp.concatenate([total[128:192, 128:256], total[192:256, 128:256]], axis=1)
    second = jnp.concatenate([total[PACK:128, :], corner, ending, zeros], axis=0)
    core = core_ref[0]

    @pl.when(core == 0)
    def _():
        keep_ref[...] = first
        give_ref[...] = second

    @pl.when(core != 0)
    def _():
        keep_ref[...] = second
        give_ref[...] = first


def gram_sums(obs_cols, obs_count, core, own, remote, pairs, sums):
    vmem = pl.BlockSpec(memory_space=pltpu.VMEM)
    smem = pl.BlockSpec(memory_space=pltpu.SMEM)
    anywhere = pl.BlockSpec(memory_space=pl.ANY)
    half = jax.ShapeDtypeStruct((PACK, 256), F32)
    return pl.pallas_call(
        gram_kernel,
        in_specs=[smem, smem, smem, anywhere, anywhere, anywhere, vmem],
        out_specs=[vmem, vmem],
        out_shape=[half, half],
        scratch_shapes=[
            pltpu.VMEM((own.shape[0] + remote.shape[0],) + own.shape[1:], BF16),
            pltpu.VMEM((2, GROUP // 2) + pairs.shape[1:], BF16),
            pltpu.VMEM((GROUP * 4, 8, 256), BF16),
            pltpu.VMEM((GROUP * 4, 8, 256), BF16),
            pltpu.VMEM((GROUP * 32, 256), BF16),
            pltpu.VMEM((GROUP * 32, 256), BF16),
            pltpu.VMEM((256, 256), F32),
            pltpu.VMEM((16, 256), F32),
            pltpu.SemaphoreType.DMA((4,)),
        ],
        compiler_params=pltpu.CompilerParams(vmem_limit_bytes=50 << 20),
        name="gram_sums",
    )(obs_cols, obs_count, core, own, remote, pairs, sums)


def dot3(left, right):
    left_high = left.astype(BF16)
    left_low = (left - left_high.astype(F32)).astype(BF16)
    right_high = right.astype(BF16)
    right_low = (right - right_high.astype(F32)).astype(BF16)
    return jnp.dot(
        jnp.concatenate([left_high, left_high, left_low], axis=1),
        jnp.concatenate([right_high, right_low, right_high], axis=0),
        preferred_element_type=F32,
    )


def apply_kernel(
    core_ref, mine_ref, other_ref, mean_ref, anom_ref, out_ref,
    levels, results, approx_ref, inverse_ref, in_sems, out_sems,
):
    lev_dev = anom_ref.shape[0]
    members = anom_ref.shape[2]
    loads = [
        pltpu.make_async_copy(anom_ref.at[v], levels.at[v], in_sems.at[v]) for v in range(lev_dev)
    ]
    for load in loads:
        load.start()
    core = core_ref[0]
    mine, other = mine_ref[...], other_ref[...]
    first = jnp.where(core == 0, mine, other)
    second = jnp.where(core == 0, other, mine)
    upper = jnp.concatenate([first, second[: 128 - PACK]], axis=0)
    packed = second[128 - PACK : 192 - PACK]
    corner = jnp.concatenate([packed[:, :128], packed[:, 128:]], axis=0)
    projection = second[192 - PACK : 193 - PACK]
    sums = second[193 - PACK : 194 - PACK]
    side = upper[:, 128:]
    gram = jnp.concatenate([upper, jnp.concatenate([side.T, corner], axis=1)], axis=0)
    gram = 0.5 * (gram + gram.T)

    numerator, obs_total = sums[:, 0:1], sums[:, 1:2]
    shift = (members - 1.0) * obs_total / numerator
    rows = lax.broadcasted_iota(jnp.int32, (members, members), 0)
    lanes = lax.broadcasted_iota(jnp.int32, (members, members), 1)
    identity = jnp.where(rows == lanes, 1.0, 0.0)
    system = gram + shift * identity
    norm = jnp.sqrt(jnp.sum(system * system, axis=(0, 1), keepdims=True))
    approx_ref[...] = system / norm
    inverse_ref[...] = identity
    lowest = jnp.minimum(jnp.sqrt(shift / norm), 1.0)[0, 0]

    def advance(scale):
        approx, inverse = approx_ref[...], inverse_ref[...]
        middle = (1.5 * scale) * identity - (0.5 * scale * scale * scale) * dot3(inverse, approx)
        approx_ref[...] = dot3(approx, middle)
        inverse_ref[...] = dot3(middle, inverse)

    def more(carried):
        turn, low = carried
        return jnp.logical_and(turn < 60, low < 0.999)

    def turn_once(carried):
        turn, low = carried
        x = jnp.maximum(low, 0.02)
        scale = 1.7323 + x * (-0.88804 + x * (-0.071549 + x * (0.385863 - 0.15965 * x)))
        scale = jnp.maximum(scale, 1.0)
        advance(scale)
        at_low = 0.5 * scale * low * (3.0 - scale * scale * low * low)
        at_one = 0.5 * scale * (3.0 - scale * scale)
        return turn + 1, jnp.minimum(at_low, at_one)

    lax.while_loop(more, turn_once, (jnp.int32(0), lowest))
    advance(1.0)
    inverse = inverse_ref[...]
    line = jnp.broadcast_to(projection, (128, members)).T
    weights = dot3(inverse, dot3(inverse, line)) / norm
    root = (jnp.sqrt((members - 1.0) / norm)) * inverse
    transform = (root + jnp.concatenate([weights, weights], axis=1)).astype(BF16)

    means = mean_ref[...].T
    stores = []
    for v in range(lev_dev):
        loads[v].wait()
        updated = jnp.dot(levels[v], transform, preferred_element_type=F32)
        results[v] = (means[:, v : v + 1] + updated).astype(BF16)
        stores.append(pltpu.make_async_copy(results.at[v], out_ref.at[v], out_sems.at[v]))
        stores[v].start()
    for store in stores:
        store.wait()


def solve_and_apply(core, mine, other, mean_state, anomalies):
    vmem = pl.BlockSpec(memory_space=pltpu.VMEM)
    anywhere = pl.BlockSpec(memory_space=pl.ANY)
    lev_dev, _, members = anomalies.shape
    return pl.pallas_call(
        apply_kernel,
        in_specs=[pl.BlockSpec(memory_space=pltpu.SMEM), vmem, vmem, vmem, anywhere],
        out_specs=anywhere,
        out_shape=jax.ShapeDtypeStruct(anomalies.shape, BF16),
        scratch_shapes=[
            pltpu.VMEM(anomalies.shape, BF16),
            pltpu.VMEM(anomalies.shape, BF16),
            pltpu.VMEM((members, members), F32),
            pltpu.VMEM((members, members), F32),
            pltpu.SemaphoreType.DMA((lev_dev,)),
            pltpu.SemaphoreType.DMA((lev_dev,)),
        ],
        compiler_params=pltpu.CompilerParams(vmem_limit_bytes=53 << 20),
        name="solve_and_apply",
    )(core, mine, other, mean_state, anomalies)


def swap(value, devices, mask):
    return lax.ppermute(value, AXES, [(d, d ^ mask) for d in range(devices)])


def sum_over(value, devices, one, two):
    arrived = [swap(value, devices, mask) for mask in (one, two, one | two)]
    return (value + arrived[0]) + (arrived[1] + arrived[2])


def per_device(
    devices, anomalies, mean_state, obs_op, innovations, obs_rinv, obs_cols, send_cols, obs_count
):
    blocks = obs_op.shape[0]
    per_block = innovations.shape[0] // blocks
    core = (lax.axis_index("lev") % 2).astype(jnp.int32).reshape(1)
    outgoing = gather_sent(send_cols, anomalies)
    remote = lax.all_to_all(outgoing, "tile", split_axis=0, concat_axis=0, tiled=True)

    rinv_blocks = obs_rinv.reshape(blocks, per_block)
    innov_blocks = innovations.reshape(blocks, per_block)
    pairs, sums, own = prepare(obs_count, obs_op, rinv_blocks, innov_blocks, anomalies)
    keep, give = gram_sums(obs_cols, obs_count, core, own, remote, pairs, sums)
    value = keep + swap(give, devices, 1)
    for one, two in ((2, 8), (32, 6), (24, 96)):
        value = sum_over(value, devices, one, two)
    other = swap(value, devices, 1)
    return solve_and_apply(core, value, other, mean_state, anomalies)


def solution(mesh):
    return jax.shard_map(
        functools.partial(per_device, mesh.size),
        mesh=mesh,
        in_specs=(
            P("lev", "tile", None),
            P("lev", "tile"),
            P(("tile", "lev"), None),
            P(("tile", "lev")),
            P(("tile", "lev")),
            P(("tile", "lev")),
            P("tile", None),
            P(("tile", "lev")),
        ),
        out_specs=P("lev", "tile", None),
        check_vma=False,
    )
```

```python
import functools

import jax
import jax.numpy as jnp
from jax import lax
from jax.experimental import pallas as pl
from jax.experimental.pallas import tpu as pltpu
from jax.sharding import PartitionSpec as P

F32 = jnp.float32
BF16 = jnp.bfloat16
AXES = ("tile", "lev")
GROUP = 128
CHUNK = 64
PACK = 88


def split3(value):
    high = value.astype(BF16)
    rest = value - high.astype(F32)
    middle = rest.astype(BF16)
    low = (rest - middle.astype(F32)).astype(BF16)
    return high, middle, low


def send_kernel(send_ref, anom_ref, out_ref, levels, table, sems):
    col_dev = anom_ref.shape[1]
    slots = out_ref.shape[0]
    steps = sems.shape[0]
    some = col_dev // steps
    copies = []
    for k in range(steps):
        part = pl.ds(k * some, some)
        copies.append(pltpu.make_async_copy(anom_ref.at[:, part], levels.at[:, part], sems.at[k]))
        copies[k].start()
    for k in range(steps):
        copies[k].wait()
        part = slice(k * some, (k + 1) * some)
        table[part] = jnp.swapaxes(levels[:, part, :], 0, 1)

    def pick(step, carried):
        for i in range(64):
            slot = step * 64 + i
            out_ref[slot] = table[send_ref[0, slot]]
        return carried

    lax.fori_loop(0, slots // 64, pick, 0)


def gather_sent(send_cols, anomalies):
    lev_dev, col_dev, members = anomalies.shape
    slots = send_cols.shape[1]
    return pl.pallas_call(
        send_kernel,
        in_specs=[pl.BlockSpec(memory_space=pltpu.SMEM), pl.BlockSpec(memory_space=pl.ANY)],
        out_specs=pl.BlockSpec(memory_space=pltpu.VMEM),
        out_shape=jax.ShapeDtypeStruct((slots, lev_dev, members), BF16),
        scratch_shapes=[
            pltpu.VMEM((lev_dev, col_dev, members), BF16),
            pltpu.VMEM((col_dev, lev_dev, members), BF16),
            pltpu.SemaphoreType.DMA((8,)),
        ],
        compiler_params=pltpu.CompilerParams(vmem_limit_bytes=60 << 20),
        name="gather_sent",
    )(send_cols, anomalies)


def prepare_kernel(
    count_ref, op_ref, rinv_ref, innov_ref, anom_ref, pair_ref, sums_ref, own_ref,
    ops, levels, expand, wide, folded, built, turned, in_sems, anom_sems, out_sems, own_sems,
):
    blocks, width = op_ref.shape
    per_block = rinv_ref.shape[1]
    points = width // per_block
    tiles = width // 128
    count = count_ref[0]
    steps = blocks // CHUNK
    loads = []
    for k in range(steps):
        part = pl.ds(k * CHUNK, CHUNK)
        loads.append(pltpu.make_async_copy(op_ref.at[part], ops.at[part], in_sems.at[k]))
        loads[k].start()
    col_dev = anom_ref.shape[1]
    some = col_dev // steps
    reads = []
    for k in range(steps):
        part = pl.ds(k * some, some)
        reads.append(
            pltpu.make_async_copy(anom_ref.at[:, part], levels.at[:, part], anom_sems.at[k])
        )
        reads[k].start()
    spread_row = lax.broadcasted_iota(jnp.int32, (2 * per_block, 256), 0)
    spread_row = jnp.where(spread_row < per_block, spread_row, spread_row - per_block) * points
    ahead = lax.broadcasted_iota(jnp.int32, (2 * per_block, 256), 1) - spread_row
    for t in range(tiles // 2):
        inside = jnp.logical_and(ahead >= -t * 256, ahead < points - t * 256)
        expand[:, t * 256 : (t + 1) * 256] = jnp.where(inside, 1.0, 0.0).astype(BF16)
    live = lax.broadcasted_iota(jnp.int32, (blocks, per_block), 0) < count
    innov = innov_ref[...]
    squares = jnp.where(live, rinv_ref[...] * innov * innov, 0.0)
    numerator = jnp.sum(squares, axis=(0, 1), keepdims=True)
    total = jnp.full((1, 1), count * per_block, jnp.int32).astype(F32)
    lane = lax.broadcasted_iota(jnp.int32, (8, 256), 1)
    sums_ref[...] = jnp.where(lane == 0, numerator, jnp.where(lane == 1, total, 0.0))
    low_half = lax.broadcasted_iota(jnp.int32, (1, 128), 1) < points
    extra_row = lax.broadcasted_iota(jnp.int32, (CHUNK // 2, 16, 128), 1)

    def store(k):
        part = pl.ds(k * (CHUNK // 2), CHUNK // 2)
        return pltpu.make_async_copy(built.at[k % 2], pair_ref.at[part], out_sems.at[k % 2])

    def store_own(k):
        part = pl.ds(k * some, some)
        return pltpu.make_async_copy(turned.at[k % 2], own_ref.at[part], own_sems.at[k % 2])

    for k in range(steps):
        start = k * CHUNK
        alive = start + lax.broadcasted_iota(jnp.int32, (CHUNK, per_block), 0) < count
        rinv = jnp.where(alive, rinv_ref[start : start + CHUNK, :], 0.0)
        factors = jnp.concatenate([jnp.sqrt(rinv), rinv * innov_ref[start : start + CHUNK, :]], 0)
        high, middle, _ = split3(factors)
        both = jnp.concatenate([high, middle], axis=1)
        loads[k].wait()
        column = jnp.zeros((CHUNK, 128), F32)
        for t in range(tiles // 2):
            lanes = slice(t * 256, (t + 1) * 256)
            spread = jnp.dot(both, expand[:, lanes], preferred_element_type=F32)
            part = ops[start : start + CHUNK, lanes].astype(F32)
            weighted = part * spread[:CHUNK]
            pulled = part * spread[CHUNK:]
            column = column + (pulled[:, :128] + pulled[:, 128:])
            wide[pl.ds(2 * t, CHUNK, stride=tiles), :] = weighted[:, :128]
            wide[pl.ds(2 * t + 1, CHUNK, stride=tiles), :] = weighted[:, 128:]
        folded[...] = column + pltpu.roll(column, points, 1)
        if k >= 2:
            store(k - 2).wait()
        slot = built.at[k % 2]
        column = jnp.where(
            low_half,
            folded[pl.ds(0, CHUNK // 2, stride=2), :],
            folded[pl.ds(1, CHUNK // 2, stride=2), :],
        )
        high, middle, low = [piece.astype(F32)[:, None, :] for piece in split3(column)]
        extra = jnp.where(extra_row == 2, low, 0.0)
        extra = jnp.where(extra_row == 1, middle, extra)
        slot[:, 128:144, :] = jnp.where(extra_row == 0, high, extra).astype(BF16)

        def pair_up(step, carried, slot=slot):
            for i in range(CHUNK // 2):
                pair = step * (CHUNK // 2) + i
                place = pl.multiple_of(pair * 2 * tiles, 2 * tiles)
                first = wide[pl.ds(place, tiles), :]
                second = wide[pl.ds(place + tiles, tiles), :]
                pieces = [
                    jnp.where(low_half, first, 0.0),
                    jnp.where(low_half, pltpu.roll(first, points, 1), 0.0),
                    jnp.where(low_half, 0.0, pltpu.roll(second, points, 1)),
                    jnp.where(low_half, 0.0, second),
                ]
                for q in range(4):
                    slot[pair, q * tiles : (q + 1) * tiles, :] = pieces[q].astype(BF16)
            return carried

        lax.fori_loop(0, 1, pair_up, 0)
        store(k).start()
        reads[k].wait()
        if k >= 2:
            store_own(k - 2).wait()
        turned[k % 2] = jnp.swapaxes(levels[:, k * some : (k + 1) * some, :], 0, 1)
        store_own(k).start()
    store_own(steps - 2).wait()
    store_own(steps - 1).wait()
    store(steps - 2).wait()
    store(steps - 1).wait()


def prepare(obs_count, obs_op, rinv_blocks, innov_blocks, anomalies):
    blocks, width = obs_op.shape
    lev_dev, col_dev, members = anomalies.shape
    steps = blocks // CHUNK
    vmem = pl.BlockSpec(memory_space=pltpu.VMEM)
    anywhere = pl.BlockSpec(memory_space=pl.ANY)
    return pl.pallas_call(
        prepare_kernel,
        in_specs=[pl.BlockSpec(memory_space=pltpu.SMEM), anywhere, vmem, vmem, anywhere],
        out_specs=[anywhere, vmem, anywhere],
        out_shape=[
            jax.ShapeDtypeStruct((blocks // 2, 144, 128), BF16),
            jax.ShapeDtypeStruct((8, 256), F32),
            jax.ShapeDtypeStruct((col_dev, lev_dev, members), BF16),
        ],
        scratch_shapes=[
            pltpu.VMEM((blocks, width), BF16),
            pltpu.VMEM(anomalies.shape, BF16),
            pltpu.VMEM((128, width), BF16),
            pltpu.VMEM((CHUNK * width // 128, 128), F32),
            pltpu.VMEM((CHUNK, 128), F32),
            pltpu.VMEM((2, CHUNK // 2, 144, 128), BF16),
            pltpu.VMEM((2, col_dev // steps, lev_dev, members), BF16),
            pltpu.SemaphoreType.DMA((steps,)),
            pltpu.SemaphoreType.DMA((steps,)),
            pltpu.SemaphoreType.DMA((2,)),
            pltpu.SemaphoreType.DMA((2,)),
        ],
        compiler_params=pltpu.CompilerParams(vmem_limit_bytes=52 << 20),
        name="prepare_operators",
    )(obs_count, obs_op, rinv_blocks, innov_blocks, anomalies)


def gram_kernel(
    cols_ref, count_ref, core_ref, own_ref, remote_ref, pair_ref, sums_ref,
    keep_ref, give_ref, table, pairs, support_a, support_b, scaled_a, scaled_b, total, pulled, sems,
):
    own_cols = own_ref.shape[0]
    group_pairs = GROUP // 2
    own = pltpu.make_async_copy(own_ref, table.at[pl.ds(0, own_cols)], sems.at[2])
    remote = pltpu.make_async_copy(
        remote_ref, table.at[pl.ds(own_cols, remote_ref.shape[0])], sems.at[3]
    )
    own.start()
    remote.start()
    groups = (count_ref[0] + GROUP - 1) // GROUP

    def fetch(g):
        part = pl.ds(g * group_pairs, group_pairs)
        return pltpu.make_async_copy(pair_ref.at[part], pairs.at[g % 2], sems.at[g % 2])

    fetch(0).start()
    total[...] = jnp.zeros_like(total)
    pulled[...] = jnp.zeros_like(pulled)
    remote.wait()
    own.wait()

    half = GROUP // 2
    most_halves = cols_ref.shape[0] // (half * 8)

    def collect(h, support):
        place = jnp.minimum(h, most_halves - 1) * (half * 8)
        for i in range(half * 8):
            support[i] = table[cols_ref[place + i]]

    def add(operators, first, support, scaled):
        extra = jnp.zeros((16, 256), F32)
        for j in range(half // 2):
            points = support[j * 16 : (j + 1) * 16].reshape(128, 256)
            images = jnp.dot(operators[first + j], points, preferred_element_type=F32)
            scaled[j * 128 : (j + 1) * 128, :] = images[:128].astype(BF16)
            extra = extra + images[128:]
        pulled[...] += extra
        rows = scaled[...]
        total[...] += lax.dot_general(
            rows, rows, (((0,), (0,)), ((), ())), preferred_element_type=F32
        )

    def step(g, carried):
        fetch(g).wait()

        @pl.when(g + 1 < groups)
        def _():
            fetch(g + 1).start()

        operators = pairs.at[g % 2]
        collect(2 * g + 1, support_b)
        add(operators, 0, support_a, scaled_a)
        collect(2 * g + 2, support_a)
        add(operators, half // 2, support_b, scaled_b)
        return carried

    collect(0, support_a)
    lax.fori_loop(0, groups, step, 0)

    projection = pulled[0:1, :] + pulled[1:2, :] + pulled[2:3, :]
    row = lax.broadcasted_iota(jnp.int32, (8, 256), 0)
    ending = jnp.where(row == 0, projection, jnp.where(row == 1, sums_ref[...], 0.0))
    zeros = jnp.zeros((8, 256), F32)
    last = pltpu.roll(total[192:256, 128:256], 64, 1)
    low_half = lax.broadcasted_iota(jnp.int32, (64, 128), 1) < 64
    side = jnp.where(low_half, last, total[64:128, 0:128])
    side = jnp.concatenate([side, total[64:128, 128:256]], axis=1)
    corner = jnp.concatenate([total[128:160, 128:256], total[160:192, 128:256]], axis=1)
    first = jnp.concatenate([total[0:64, :], side[: PACK - 64]], axis=0)
    second = jnp.concatenate([side[PACK - 64 :], corner, ending, zeros], axis=0)
    core = core_ref[0]

    @pl.when(core == 0)
    def _():
        keep_ref[...] = first
        give_ref[...] = second

    @pl.when(core != 0)
    def _():
        keep_ref[...] = second
        give_ref[...] = first


def gram_sums(obs_cols, obs_count, core, own, remote, pairs, sums):
    vmem = pl.BlockSpec(memory_space=pltpu.VMEM)
    smem = pl.BlockSpec(memory_space=pltpu.SMEM)
    anywhere = pl.BlockSpec(memory_space=pl.ANY)
    half = jax.ShapeDtypeStruct((PACK, 256), F32)
    return pl.pallas_call(
        gram_kernel,
        in_specs=[smem, smem, smem, anywhere, anywhere, anywhere, vmem],
        out_specs=[vmem, vmem],
        out_shape=[half, half],
        scratch_shapes=[
            pltpu.VMEM((own.shape[0] + remote.shape[0],) + own.shape[1:], BF16),
            pltpu.VMEM((2, GROUP // 2) + pairs.shape[1:], BF16),
            pltpu.VMEM((GROUP * 4, 8, 256), BF16),
            pltpu.VMEM((GROUP * 4, 8, 256), BF16),
            pltpu.VMEM((GROUP * 32, 256), BF16),
            pltpu.VMEM((GROUP * 32, 256), BF16),
            pltpu.VMEM((256, 256), F32),
            pltpu.VMEM((16, 256), F32),
            pltpu.SemaphoreType.DMA((4,)),
        ],
        compiler_params=pltpu.CompilerParams(vmem_limit_bytes=50 << 20),
        name="gram_sums",
    )(obs_cols, obs_count, core, own, remote, pairs, sums)


def dot3(left, right):
    left_high = left.astype(BF16)
    left_low = (left - left_high.astype(F32)).astype(BF16)
    right_high = right.astype(BF16)
    right_low = (right - right_high.astype(F32)).astype(BF16)
    return jnp.dot(
        jnp.concatenate([left_high, left_high, left_low], axis=1),
        jnp.concatenate([right_high, right_low, right_high], axis=0),
        preferred_element_type=F32,
    )


def apply_kernel(
    core_ref, mine_ref, other_ref, mean_ref, anom_ref, out_ref,
    levels, results, means, approx_ref, inverse_ref, in_sems, out_sems,
):
    lev_dev = anom_ref.shape[0]
    members = anom_ref.shape[2]
    loads = [
        pltpu.make_async_copy(anom_ref.at[v], levels.at[v], in_sems.at[v]) for v in range(lev_dev)
    ]
    for load in loads:
        load.start()
    core = core_ref[0]
    mine, other = mine_ref[...], other_ref[...]
    packed = jnp.concatenate(
        [jnp.where(core == 0, mine, other), jnp.where(core == 0, other, mine)], axis=0
    )
    side = packed[64:128]
    corner = jnp.concatenate([packed[128:160, :128], packed[128:160, 128:]], axis=0)
    corner = jnp.concatenate([corner, pltpu.roll(side[:, :128], 64, 1)], axis=0)
    corner = jnp.concatenate([jnp.zeros((128, 128), F32), corner], axis=1)
    upper = jnp.concatenate([packed[0:128], corner], axis=0)
    lower = upper.T
    rows = lax.broadcasted_iota(jnp.int32, (members, members), 0)
    lanes = lax.broadcasted_iota(jnp.int32, (members, members), 1)
    row_block = lax.shift_right_logical(rows, 6)
    lane_block = lax.shift_right_logical(lanes, 6)
    gram = jnp.where(
        lane_block > row_block,
        upper,
        jnp.where(lane_block < row_block, lower, 0.5 * (upper + lower)),
    )
    projection = packed[160:161]
    sums = packed[161:162]
    means[...] = mean_ref[...].T

    numerator, obs_total = sums[:, 0:1], sums[:, 1:2]
    shift = (members - 1.0) * obs_total / numerator
    identity = jnp.where(rows == lanes, 1.0, 0.0)
    system = gram + shift * identity
    norm = jnp.sqrt(jnp.sum(system * system, axis=(0, 1), keepdims=True))
    approx_ref[...] = system / norm
    inverse_ref[...] = identity
    lowest = jnp.minimum(jnp.sqrt(shift / norm), 1.0)[0, 0]

    def advance(scale):
        approx, inverse = approx_ref[...], inverse_ref[...]
        middle = (1.5 * scale) * identity - (0.5 * scale * scale * scale) * dot3(inverse, approx)
        approx_ref[...] = dot3(approx, middle)
        inverse_ref[...] = dot3(middle, inverse)

    def more(carried):
        turn, low = carried
        return jnp.logical_and(turn < 60, low < 0.999)

    def turn_once(carried):
        turn, low = carried
        x = jnp.maximum(low, 0.02)
        scale = 1.7323 + x * (-0.88804 + x * (-0.071549 + x * (0.385863 - 0.15965 * x)))
        scale = jnp.maximum(scale, 1.0)
        advance(scale)
        at_low = 0.5 * scale * low * (3.0 - scale * scale * low * low)
        at_one = 0.5 * scale * (3.0 - scale * scale)
        return turn + 1, jnp.minimum(at_low, at_one)

    lax.while_loop(more, turn_once, (jnp.int32(0), lowest))
    advance(1.0)
    inverse = inverse_ref[...]
    line = jnp.broadcast_to(projection, (128, members)).T
    weights = dot3(inverse, dot3(inverse, line)) / norm
    root = (jnp.sqrt((members - 1.0) / norm)) * inverse
    transform = (root + jnp.concatenate([weights, weights], axis=1)).astype(BF16)

    stores = []
    for v in range(lev_dev):
        loads[v].wait()
        updated = jnp.dot(levels[v], transform, preferred_element_type=F32)
        results[v] = (means[:, v : v + 1] + updated).astype(BF16)
        stores.append(pltpu.make_async_copy(results.at[v], out_ref.at[v], out_sems.at[v]))
        stores[v].start()
    for store in stores:
        store.wait()


def solve_and_apply(core, mine, other, mean_state, anomalies):
    vmem = pl.BlockSpec(memory_space=pltpu.VMEM)
    anywhere = pl.BlockSpec(memory_space=pl.ANY)
    lev_dev, col_dev, members = anomalies.shape
    return pl.pallas_call(
        apply_kernel,
        in_specs=[pl.BlockSpec(memory_space=pltpu.SMEM), vmem, vmem, vmem, anywhere],
        out_specs=anywhere,
        out_shape=jax.ShapeDtypeStruct(anomalies.shape, BF16),
        scratch_shapes=[
            pltpu.VMEM(anomalies.shape, BF16),
            pltpu.VMEM(anomalies.shape, BF16),
            pltpu.VMEM((col_dev, lev_dev), F32),
            pltpu.VMEM((members, members), F32),
            pltpu.VMEM((members, members), F32),
            pltpu.SemaphoreType.DMA((lev_dev,)),
            pltpu.SemaphoreType.DMA((lev_dev,)),
        ],
        compiler_params=pltpu.CompilerParams(vmem_limit_bytes=53 << 20),
        name="solve_and_apply",
    )(core, mine, other, mean_state, anomalies)


def swap(value, devices, mask):
    return lax.ppermute(value, AXES, [(d, d ^ mask) for d in range(devices)])


def sum_over(value, devices, one, two):
    arrived = [swap(value, devices, mask) for mask in (one, two, one | two)]
    return (value + arrived[0]) + (arrived[1] + arrived[2])


def per_device(
    devices, anomalies, mean_state, obs_op, innovations, obs_rinv, obs_cols, send_cols, obs_count
):
    blocks = obs_op.shape[0]
    per_block = innovations.shape[0] // blocks
    core = (lax.axis_index("lev") % 2).astype(jnp.int32).reshape(1)
    outgoing = gather_sent(send_cols, anomalies)
    remote = lax.all_to_all(outgoing, "tile", split_axis=0, concat_axis=0, tiled=True)

    rinv_blocks = obs_rinv.reshape(blocks, per_block)
    innov_blocks = innovations.reshape(blocks, per_block)
    pairs, sums, own = prepare(obs_count, obs_op, rinv_blocks, innov_blocks, anomalies)
    keep, give = gram_sums(obs_cols, obs_count, core, own, remote, pairs, sums)
    value = keep + swap(give, devices, 1)
    for one, two in ((2, 8), (32, 6), (24, 96)):
        value = sum_over(value, devices, one, two)
    other = swap(value, devices, 1)
    return solve_and_apply(core, value, other, mean_state, anomalies)


def solution(mesh):
    return jax.shard_map(
        functools.partial(per_device, mesh.size),
        mesh=mesh,
        in_specs=(
            P("lev", "tile", None),
            P("lev", "tile"),
            P(("tile", "lev"), None),
            P(("tile", "lev")),
            P(("tile", "lev")),
            P(("tile", "lev")),
            P("tile", None),
            P(("tile", "lev")),
        ),
        out_specs=P("lev", "tile", None),
        check_vma=False,
    )
```

```python
import functools

import jax
import jax.numpy as jnp
from jax import lax
from jax.experimental import pallas as pl
from jax.experimental.pallas import tpu as pltpu
from jax.sharding import PartitionSpec as P

F32 = jnp.float32
BF16 = jnp.bfloat16
AXES = ("tile", "lev")
GROUP = 128
CHUNK = 64
PACK = 88


def split3(value):
    high = value.astype(BF16)
    rest = value - high.astype(F32)
    middle = rest.astype(BF16)
    low = (rest - middle.astype(F32)).astype(BF16)
    return high, middle, low


def send_kernel(send_ref, anom_ref, out_ref, levels, table, picked, sems, out_sems):
    col_dev = anom_ref.shape[1]
    slots = out_ref.shape[0]
    steps = sems.shape[0]
    some = col_dev // steps
    copies = []
    for k in range(steps):
        part = pl.ds(k * some, some)
        copies.append(pltpu.make_async_copy(anom_ref.at[:, part], levels.at[:, part], sems.at[k]))
        copies[k].start()
    for k in range(steps):
        copies[k].wait()
        part = slice(k * some, (k + 1) * some)
        table[part] = jnp.swapaxes(levels[:, part, :], 0, 1)

    batch = slots // 6
    stores = []
    for k in range(6):
        for i in range(batch):
            slot = k * batch + i
            picked[slot] = table[send_ref[0, slot]]
        part = pl.ds(k * batch, batch)
        stores.append(pltpu.make_async_copy(picked.at[part], out_ref.at[part], out_sems.at[k]))
        stores[k].start()
    for store in stores:
        store.wait()


def gather_sent(send_cols, anomalies):
    lev_dev, col_dev, members = anomalies.shape
    slots = send_cols.shape[1]
    return pl.pallas_call(
        send_kernel,
        in_specs=[pl.BlockSpec(memory_space=pltpu.SMEM), pl.BlockSpec(memory_space=pl.ANY)],
        out_specs=pl.BlockSpec(memory_space=pl.ANY),
        out_shape=jax.ShapeDtypeStruct((slots, lev_dev, members), BF16),
        scratch_shapes=[
            pltpu.VMEM((lev_dev, col_dev, members), BF16),
            pltpu.VMEM((col_dev, lev_dev, members), BF16),
            pltpu.VMEM((slots, lev_dev, members), BF16),
            pltpu.SemaphoreType.DMA((8,)),
            pltpu.SemaphoreType.DMA((6,)),
        ],
        compiler_params=pltpu.CompilerParams(vmem_limit_bytes=60 << 20),
        name="gather_sent",
    )(send_cols, anomalies)


def prepare_kernel(
    count_ref, op_ref, rinv_ref, innov_ref, anom_ref, pair_ref, sums_ref, own_ref,
    ops, levels, expand, wide, folded, built, turned, in_sems, anom_sems, out_sems, own_sems,
):
    blocks, width = op_ref.shape
    per_block = rinv_ref.shape[1]
    points = width // per_block
    tiles = width // 128
    count = count_ref[0]
    steps = blocks // CHUNK
    loads = []
    for k in range(steps):
        part = pl.ds(k * CHUNK, CHUNK)
        loads.append(pltpu.make_async_copy(op_ref.at[part], ops.at[part], in_sems.at[k]))
        loads[k].start()
    col_dev = anom_ref.shape[1]
    some = col_dev // steps
    reads = []
    for k in range(steps):
        part = pl.ds(k * some, some)
        reads.append(
            pltpu.make_async_copy(anom_ref.at[:, part], levels.at[:, part], anom_sems.at[k])
        )
        reads[k].start()
    spread_row = lax.broadcasted_iota(jnp.int32, (2 * per_block, 256), 0)
    spread_row = jnp.where(spread_row < per_block, spread_row, spread_row - per_block) * points
    ahead = lax.broadcasted_iota(jnp.int32, (2 * per_block, 256), 1) - spread_row
    for t in range(tiles // 2):
        inside = jnp.logical_and(ahead >= -t * 256, ahead < points - t * 256)
        expand[:, t * 256 : (t + 1) * 256] = jnp.where(inside, 1.0, 0.0).astype(BF16)
    live = lax.broadcasted_iota(jnp.int32, (blocks, per_block), 0) < count
    innov = innov_ref[...]
    squares = jnp.where(live, rinv_ref[...] * innov * innov, 0.0)
    numerator = jnp.sum(squares, axis=(0, 1), keepdims=True)
    total = jnp.full((1, 1), count * per_block, jnp.int32).astype(F32)
    lane = lax.broadcasted_iota(jnp.int32, (8, 256), 1)
    sums_ref[...] = jnp.where(lane == 0, numerator, jnp.where(lane == 1, total, 0.0))
    low_half = lax.broadcasted_iota(jnp.int32, (1, 128), 1) < points
    extra_row = lax.broadcasted_iota(jnp.int32, (CHUNK // 2, 16, 128), 1)

    def store(k):
        part = pl.ds(k * (CHUNK // 2), CHUNK // 2)
        return pltpu.make_async_copy(built.at[k % 2], pair_ref.at[part], out_sems.at[k % 2])

    def store_own(k):
        part = pl.ds(k * some, some)
        return pltpu.make_async_copy(turned.at[k % 2], own_ref.at[part], own_sems.at[k % 2])

    for k in range(steps):
        start = k * CHUNK
        alive = start + lax.broadcasted_iota(jnp.int32, (CHUNK, per_block), 0) < count
        rinv = jnp.where(alive, rinv_ref[start : start + CHUNK, :], 0.0)
        factors = jnp.concatenate([jnp.sqrt(rinv), rinv * innov_ref[start : start + CHUNK, :]], 0)
        high, middle, _ = split3(factors)
        both = jnp.concatenate([high, middle], axis=1)
        loads[k].wait()
        column = jnp.zeros((CHUNK, 128), F32)
        for t in range(tiles // 2):
            lanes = slice(t * 256, (t + 1) * 256)
            spread = jnp.dot(both, expand[:, lanes], preferred_element_type=F32)
            part = ops[start : start + CHUNK, lanes].astype(F32)
            weighted = part * spread[:CHUNK]
            pulled = part * spread[CHUNK:]
            column = column + (pulled[:, :128] + pulled[:, 128:])
            wide[pl.ds(2 * t, CHUNK, stride=tiles), :] = weighted[:, :128]
            wide[pl.ds(2 * t + 1, CHUNK, stride=tiles), :] = weighted[:, 128:]
        folded[...] = column + pltpu.roll(column, points, 1)
        if k >= 2:
            store(k - 2).wait()
        slot = built.at[k % 2]
        column = jnp.where(
            low_half,
            folded[pl.ds(0, CHUNK // 2, stride=2), :],
            folded[pl.ds(1, CHUNK // 2, stride=2), :],
        )
        high, middle, low = [piece.astype(F32)[:, None, :] for piece in split3(column)]
        extra = jnp.where(extra_row == 2, low, 0.0)
        extra = jnp.where(extra_row == 1, middle, extra)
        slot[:, 128:144, :] = jnp.where(extra_row == 0, high, extra).astype(BF16)

        def pair_up(step, carried, slot=slot):
            for i in range(CHUNK // 2):
                pair = step * (CHUNK // 2) + i
                place = pl.multiple_of(pair * 2 * tiles, 2 * tiles)
                first = wide[pl.ds(place, tiles), :]
                second = wide[pl.ds(place + tiles, tiles), :]
                pieces = [
                    jnp.where(low_half, first, 0.0),
                    jnp.where(low_half, pltpu.roll(first, points, 1), 0.0),
                    jnp.where(low_half, 0.0, pltpu.roll(second, points, 1)),
                    jnp.where(low_half, 0.0, second),
                ]
                for q in range(4):
                    slot[pair, q * tiles : (q + 1) * tiles, :] = pieces[q].astype(BF16)
            return carried

        lax.fori_loop(0, 1, pair_up, 0)
        store(k).start()
        reads[k].wait()
        if k >= 2:
            store_own(k - 2).wait()
        turned[k % 2] = jnp.swapaxes(levels[:, k * some : (k + 1) * some, :], 0, 1)
        store_own(k).start()
    store_own(steps - 2).wait()
    store_own(steps - 1).wait()
    store(steps - 2).wait()
    store(steps - 1).wait()


def prepare(obs_count, obs_op, rinv_blocks, innov_blocks, anomalies):
    blocks, width = obs_op.shape
    lev_dev, col_dev, members = anomalies.shape
    steps = blocks // CHUNK
    vmem = pl.BlockSpec(memory_space=pltpu.VMEM)
    anywhere = pl.BlockSpec(memory_space=pl.ANY)
    return pl.pallas_call(
        prepare_kernel,
        in_specs=[pl.BlockSpec(memory_space=pltpu.SMEM), anywhere, vmem, vmem, anywhere],
        out_specs=[anywhere, vmem, anywhere],
        out_shape=[
            jax.ShapeDtypeStruct((blocks // 2, 144, 128), BF16),
            jax.ShapeDtypeStruct((8, 256), F32),
            jax.ShapeDtypeStruct((col_dev, lev_dev, members), BF16),
        ],
        scratch_shapes=[
            pltpu.VMEM((blocks, width), BF16),
            pltpu.VMEM(anomalies.shape, BF16),
            pltpu.VMEM((128, width), BF16),
            pltpu.VMEM((CHUNK * width // 128, 128), F32),
            pltpu.VMEM((CHUNK, 128), F32),
            pltpu.VMEM((2, CHUNK // 2, 144, 128), BF16),
            pltpu.VMEM((2, col_dev // steps, lev_dev, members), BF16),
            pltpu.SemaphoreType.DMA((steps,)),
            pltpu.SemaphoreType.DMA((steps,)),
            pltpu.SemaphoreType.DMA((2,)),
            pltpu.SemaphoreType.DMA((2,)),
        ],
        compiler_params=pltpu.CompilerParams(vmem_limit_bytes=52 << 20),
        name="prepare_operators",
    )(obs_count, obs_op, rinv_blocks, innov_blocks, anomalies)


def gram_kernel(
    cols_ref, count_ref, core_ref, own_ref, remote_ref, pair_ref, sums_ref,
    keep_ref, give_ref, table, pairs, support_a, support_b, scaled_a, scaled_b, total, pulled, sems,
):
    own_cols = own_ref.shape[0]
    group_pairs = GROUP // 2
    own = pltpu.make_async_copy(own_ref, table.at[pl.ds(0, own_cols)], sems.at[2])
    remote = pltpu.make_async_copy(
        remote_ref, table.at[pl.ds(own_cols, remote_ref.shape[0])], sems.at[3]
    )
    own.start()
    remote.start()
    groups = (count_ref[0] + GROUP - 1) // GROUP

    def fetch(g):
        part = pl.ds(g * group_pairs, group_pairs)
        return pltpu.make_async_copy(pair_ref.at[part], pairs.at[g % 2], sems.at[g % 2])

    fetch(0).start()
    total[...] = jnp.zeros_like(total)
    pulled[...] = jnp.zeros_like(pulled)
    remote.wait()
    own.wait()

    half = GROUP // 2
    most_halves = cols_ref.shape[0] // (half * 8)

    def collect(h, support):
        place = jnp.minimum(h, most_halves - 1) * (half * 8)
        for i in range(half * 8):
            support[i] = table[cols_ref[place + i]]

    def add(operators, first, support, scaled):
        extra = jnp.zeros((16, 256), F32)
        for j in range(half // 2):
            points = support[j * 16 : (j + 1) * 16].reshape(128, 256)
            images = jnp.dot(operators[first + j], points, preferred_element_type=F32)
            scaled[j * 128 : (j + 1) * 128, :] = images[:128].astype(BF16)
            extra = extra + images[128:]
        pulled[...] += extra
        rows = scaled[...]
        total[...] += lax.dot_general(
            rows, rows, (((0,), (0,)), ((), ())), preferred_element_type=F32
        )

    def step(g, carried):
        fetch(g).wait()

        @pl.when(g + 1 < groups)
        def _():
            fetch(g + 1).start()

        operators = pairs.at[g % 2]
        collect(2 * g + 1, support_b)
        add(operators, 0, support_a, scaled_a)
        collect(2 * g + 2, support_a)
        add(operators, half // 2, support_b, scaled_b)
        return carried

    collect(0, support_a)
    lax.fori_loop(0, groups, step, 0)

    projection = pulled[0:1, :] + pulled[1:2, :] + pulled[2:3, :]
    row = lax.broadcasted_iota(jnp.int32, (8, 256), 0)
    ending = jnp.where(row == 0, projection, jnp.where(row == 1, sums_ref[...], 0.0))
    zeros = jnp.zeros((8, 256), F32)
    last = pltpu.roll(total[192:256, 128:256], 64, 1)
    low_half = lax.broadcasted_iota(jnp.int32, (64, 128), 1) < 64
    side = jnp.where(low_half, last, total[64:128, 0:128])
    side = jnp.concatenate([side, total[64:128, 128:256]], axis=1)
    corner = jnp.concatenate([total[128:160, 128:256], total[160:192, 128:256]], axis=1)
    first = jnp.concatenate([total[0:64, :], side[: PACK - 64]], axis=0)
    second = jnp.concatenate([side[PACK - 64 :], corner, ending, zeros], axis=0)
    core = core_ref[0]

    @pl.when(core == 0)
    def _():
        keep_ref[...] = first
        give_ref[...] = second

    @pl.when(core != 0)
    def _():
        keep_ref[...] = second
        give_ref[...] = first


def gram_sums(obs_cols, obs_count, core, own, remote, pairs, sums):
    vmem = pl.BlockSpec(memory_space=pltpu.VMEM)
    smem = pl.BlockSpec(memory_space=pltpu.SMEM)
    anywhere = pl.BlockSpec(memory_space=pl.ANY)
    half = jax.ShapeDtypeStruct((PACK, 256), F32)
    return pl.pallas_call(
        gram_kernel,
        in_specs=[smem, smem, smem, anywhere, anywhere, anywhere, vmem],
        out_specs=[vmem, vmem],
        out_shape=[half, half],
        scratch_shapes=[
            pltpu.VMEM((own.shape[0] + remote.shape[0],) + own.shape[1:], BF16),
            pltpu.VMEM((2, GROUP // 2) + pairs.shape[1:], BF16),
            pltpu.VMEM((GROUP * 4, 8, 256), BF16),
            pltpu.VMEM((GROUP * 4, 8, 256), BF16),
            pltpu.VMEM((GROUP * 32, 256), BF16),
            pltpu.VMEM((GROUP * 32, 256), BF16),
            pltpu.VMEM((256, 256), F32),
            pltpu.VMEM((16, 256), F32),
            pltpu.SemaphoreType.DMA((4,)),
        ],
        compiler_params=pltpu.CompilerParams(vmem_limit_bytes=50 << 20),
        name="gram_sums",
    )(obs_cols, obs_count, core, own, remote, pairs, sums)


def dot3(left, right):
    left_high = left.astype(BF16)
    left_low = (left - left_high.astype(F32)).astype(BF16)
    right_high = right.astype(BF16)
    right_low = (right - right_high.astype(F32)).astype(BF16)
    return jnp.dot(
        jnp.concatenate([left_high, left_high, left_low], axis=1),
        jnp.concatenate([right_high, right_low, right_high], axis=0),
        preferred_element_type=F32,
    )


def apply_kernel(
    core_ref, mine_ref, other_ref, mean_ref, anom_ref, out_ref,
    levels, results, means, approx_ref, inverse_ref, in_sems, out_sems,
):
    lev_dev = anom_ref.shape[0]
    members = anom_ref.shape[2]
    loads = [
        pltpu.make_async_copy(anom_ref.at[v], levels.at[v], in_sems.at[v]) for v in range(lev_dev)
    ]
    for load in loads:
        load.start()
    core = core_ref[0]
    mine, other = mine_ref[...], other_ref[...]
    packed = jnp.concatenate(
        [jnp.where(core == 0, mine, other), jnp.where(core == 0, other, mine)], axis=0
    )
    side = packed[64:128]
    corner = jnp.concatenate([packed[128:160, :128], packed[128:160, 128:]], axis=0)
    corner = jnp.concatenate([corner, pltpu.roll(side[:, :128], 64, 1)], axis=0)
    corner = jnp.concatenate([jnp.zeros((128, 128), F32), corner], axis=1)
    upper = jnp.concatenate([packed[0:128], corner], axis=0)
    lower = upper.T
    rows = lax.broadcasted_iota(jnp.int32, (members, members), 0)
    lanes = lax.broadcasted_iota(jnp.int32, (members, members), 1)
    row_block = lax.shift_right_logical(rows, 6)
    lane_block = lax.shift_right_logical(lanes, 6)
    gram = jnp.where(
        lane_block > row_block,
        upper,
        jnp.where(lane_block < row_block, lower, 0.5 * (upper + lower)),
    )
    projection = packed[160:161]
    sums = packed[161:162]
    means[...] = mean_ref[...].T

    numerator, obs_total = sums[:, 0:1], sums[:, 1:2]
    shift = (members - 1.0) * obs_total / numerator
    identity = jnp.where(rows == lanes, 1.0, 0.0)
    system = gram + shift * identity
    norm = jnp.sqrt(jnp.sum(system * system, axis=(0, 1), keepdims=True))
    lowest = jnp.minimum(jnp.sqrt(shift / norm), 1.0)[0, 0]

    def factor(scale, product):
        return (1.5 * scale) * identity - (0.5 * scale * scale * scale) * product

    def next_scale(low):
        x = jnp.maximum(low, 0.02)
        scale = 1.7323 + x * (-0.88804 + x * (-0.071549 + x * (0.385863 - 0.15965 * x)))
        scale = jnp.maximum(scale, 1.0)
        at_low = 0.5 * scale * low * (3.0 - scale * scale * low * low)
        at_one = 0.5 * scale * (3.0 - scale * scale)
        return scale, jnp.minimum(at_low, at_one)

    def more(carried):
        turn, low = carried
        return jnp.logical_and(turn < 60, low < 0.999)

    def advance(carried):
        turn, low = carried
        scale, low = next_scale(low)
        approx, inverse = approx_ref[...], inverse_ref[...]
        middle = factor(scale, dot3(inverse, approx))
        approx_ref[...] = dot3(approx, middle)
        inverse_ref[...] = dot3(middle, inverse)
        return turn + 1, low

    start = system / norm
    scale, lowest = next_scale(lowest)
    middle = factor(scale, start)
    approx_ref[...] = dot3(start, middle)
    inverse_ref[...] = middle
    lax.while_loop(more, advance, (jnp.int32(0), lowest))
    inverse = inverse_ref[...]
    inverse = dot3(factor(1.0, dot3(inverse, approx_ref[...])), inverse)
    line = jnp.broadcast_to(projection, (128, members)).T
    weights = dot3(inverse, dot3(inverse, line)) / norm
    root = (jnp.sqrt((members - 1.0) / norm)) * inverse
    transform = (root + jnp.concatenate([weights, weights], axis=1)).astype(BF16)

    stores = []
    for v in range(lev_dev):
        loads[v].wait()
        updated = jnp.dot(levels[v], transform, preferred_element_type=F32)
        results[v] = (means[:, v : v + 1] + updated).astype(BF16)
        stores.append(pltpu.make_async_copy(results.at[v], out_ref.at[v], out_sems.at[v]))
        stores[v].start()
    for store in stores:
        store.wait()


def solve_and_apply(core, mine, other, mean_state, anomalies):
    vmem = pl.BlockSpec(memory_space=pltpu.VMEM)
    anywhere = pl.BlockSpec(memory_space=pl.ANY)
    lev_dev, col_dev, members = anomalies.shape
    return pl.pallas_call(
        apply_kernel,
        in_specs=[pl.BlockSpec(memory_space=pltpu.SMEM), vmem, vmem, vmem, anywhere],
        out_specs=anywhere,
        out_shape=jax.ShapeDtypeStruct(anomalies.shape, BF16),
        scratch_shapes=[
            pltpu.VMEM(anomalies.shape, BF16),
            pltpu.VMEM(anomalies.shape, BF16),
            pltpu.VMEM((col_dev, lev_dev), F32),
            pltpu.VMEM((members, members), F32),
            pltpu.VMEM((members, members), F32),
            pltpu.SemaphoreType.DMA((lev_dev,)),
            pltpu.SemaphoreType.DMA((lev_dev,)),
        ],
        compiler_params=pltpu.CompilerParams(vmem_limit_bytes=53 << 20),
        name="solve_and_apply",
    )(core, mine, other, mean_state, anomalies)


def swap(value, devices, mask):
    return lax.ppermute(value, AXES, [(d, d ^ mask) for d in range(devices)])


def sum_over(value, devices, one, two):
    arrived = [swap(value, devices, mask) for mask in (one, two, one | two)]
    return (value + arrived[0]) + (arrived[1] + arrived[2])


def per_device(
    devices, anomalies, mean_state, obs_op, innovations, obs_rinv, obs_cols, send_cols, obs_count
):
    blocks = obs_op.shape[0]
    per_block = innovations.shape[0] // blocks
    core = (lax.axis_index("lev") % 2).astype(jnp.int32).reshape(1)
    outgoing = gather_sent(send_cols, anomalies)
    remote = lax.all_to_all(outgoing, "tile", split_axis=0, concat_axis=0, tiled=True)

    rinv_blocks = obs_rinv.reshape(blocks, per_block)
    innov_blocks = innovations.reshape(blocks, per_block)
    pairs, sums, own = prepare(obs_count, obs_op, rinv_blocks, innov_blocks, anomalies)
    keep, give = gram_sums(obs_cols, obs_count, core, own, remote, pairs, sums)
    value = keep + swap(give, devices, 1)
    for one, two in ((2, 8), (32, 6), (24, 96)):
        value = sum_over(value, devices, one, two)
    other = swap(value, devices, 1)
    return solve_and_apply(core, value, other, mean_state, anomalies)


def solution(mesh):
    return jax.shard_map(
        functools.partial(per_device, mesh.size),
        mesh=mesh,
        in_specs=(
            P("lev", "tile", None),
            P("lev", "tile"),
            P(("tile", "lev"), None),
            P(("tile", "lev")),
            P(("tile", "lev")),
            P(("tile", "lev")),
            P("tile", None),
            P(("tile", "lev")),
        ),
        out_specs=P("lev", "tile", None),
        check_vma=False,
    )
```

```python
import functools

import jax
import jax.numpy as jnp
from jax import lax
from jax.experimental import pallas as pl
from jax.experimental.pallas import tpu as pltpu
from jax.sharding import PartitionSpec as P

F32 = jnp.float32
BF16 = jnp.bfloat16
AXES = ("tile", "lev")
GROUP = 128
CHUNK = 64
PACK = 72


def split3(value):
    high = value.astype(BF16)
    rest = value - high.astype(F32)
    middle = rest.astype(BF16)
    low = (rest - middle.astype(F32)).astype(BF16)
    return high, middle, low


def send_kernel(send_ref, anom_ref, out_ref, levels, table, picked, sems, out_sems):
    col_dev = anom_ref.shape[1]
    slots = out_ref.shape[0]
    steps = sems.shape[0]
    some = col_dev // steps
    copies = []
    for k in range(steps):
        part = pl.ds(k * some, some)
        copies.append(pltpu.make_async_copy(anom_ref.at[:, part], levels.at[:, part], sems.at[k]))
        copies[k].start()
    for k in range(steps):
        copies[k].wait()
        part = slice(k * some, (k + 1) * some)
        table[part] = jnp.swapaxes(levels[:, part, :], 0, 1)

    batch = slots // 6
    stores = []
    for k in range(6):
        for i in range(batch):
            slot = k * batch + i
            picked[slot] = table[send_ref[0, slot]]
        part = pl.ds(k * batch, batch)
        stores.append(pltpu.make_async_copy(picked.at[part], out_ref.at[part], out_sems.at[k]))
        stores[k].start()
    for store in stores:
        store.wait()


def gather_sent(send_cols, anomalies):
    lev_dev, col_dev, members = anomalies.shape
    slots = send_cols.shape[1]
    return pl.pallas_call(
        send_kernel,
        in_specs=[pl.BlockSpec(memory_space=pltpu.SMEM), pl.BlockSpec(memory_space=pl.ANY)],
        out_specs=pl.BlockSpec(memory_space=pl.ANY),
        out_shape=jax.ShapeDtypeStruct((slots, lev_dev, members), BF16),
        scratch_shapes=[
            pltpu.VMEM((lev_dev, col_dev, members), BF16),
            pltpu.VMEM((col_dev, lev_dev, members), BF16),
            pltpu.VMEM((slots, lev_dev, members), BF16),
            pltpu.SemaphoreType.DMA((8,)),
            pltpu.SemaphoreType.DMA((6,)),
        ],
        compiler_params=pltpu.CompilerParams(vmem_limit_bytes=60 << 20),
        name="gather_sent",
    )(send_cols, anomalies)


def prepare_kernel(
    count_ref, op_ref, rinv_ref, innov_ref, anom_ref, pair_ref, sums_ref, own_ref,
    ops, levels, expand, wide, folded, built, turned, in_sems, anom_sems, out_sems, own_sems,
):
    blocks, width = op_ref.shape
    per_block = rinv_ref.shape[1]
    points = width // per_block
    tiles = width // 128
    count = count_ref[0]
    steps = blocks // CHUNK
    loads = []
    for k in range(steps):
        part = pl.ds(k * CHUNK, CHUNK)
        loads.append(pltpu.make_async_copy(op_ref.at[part], ops.at[part], in_sems.at[k]))
        loads[k].start()
    col_dev = anom_ref.shape[1]
    some = col_dev // steps
    reads = []
    for k in range(steps):
        part = pl.ds(k * some, some)
        reads.append(
            pltpu.make_async_copy(anom_ref.at[:, part], levels.at[:, part], anom_sems.at[k])
        )
        reads[k].start()
    spread_row = lax.broadcasted_iota(jnp.int32, (2 * per_block, 256), 0)
    spread_row = jnp.where(spread_row < per_block, spread_row, spread_row - per_block) * points
    ahead = lax.broadcasted_iota(jnp.int32, (2 * per_block, 256), 1) - spread_row
    for t in range(tiles // 2):
        inside = jnp.logical_and(ahead >= -t * 256, ahead < points - t * 256)
        expand[:, t * 256 : (t + 1) * 256] = jnp.where(inside, 1.0, 0.0).astype(BF16)
    live = lax.broadcasted_iota(jnp.int32, (blocks, per_block), 0) < count
    innov = innov_ref[...]
    squares = jnp.where(live, rinv_ref[...] * innov * innov, 0.0)
    numerator = jnp.sum(squares, axis=(0, 1), keepdims=True)
    total = jnp.full((1, 1), count * per_block, jnp.int32).astype(F32)
    lane = lax.broadcasted_iota(jnp.int32, (8, 256), 1)
    sums_ref[...] = jnp.where(lane == 0, numerator, jnp.where(lane == 1, total, 0.0))
    low_half = lax.broadcasted_iota(jnp.int32, (1, 128), 1) < points
    extra_row = lax.broadcasted_iota(jnp.int32, (CHUNK // 2, 16, 128), 1)

    def store(k):
        part = pl.ds(k * (CHUNK // 2), CHUNK // 2)
        return pltpu.make_async_copy(built.at[k % 2], pair_ref.at[part], out_sems.at[k % 2])

    def store_own(k):
        part = pl.ds(k * some, some)
        return pltpu.make_async_copy(turned.at[k % 2], own_ref.at[part], own_sems.at[k % 2])

    for k in range(steps):
        start = k * CHUNK
        alive = start + lax.broadcasted_iota(jnp.int32, (CHUNK, per_block), 0) < count
        rinv = jnp.where(alive, rinv_ref[start : start + CHUNK, :], 0.0)
        factors = jnp.concatenate([jnp.sqrt(rinv), rinv * innov_ref[start : start + CHUNK, :]], 0)
        high, middle, _ = split3(factors)
        both = jnp.concatenate([high, middle], axis=1)
        loads[k].wait()
        column = jnp.zeros((CHUNK, 128), F32)
        for t in range(tiles // 2):
            lanes = slice(t * 256, (t + 1) * 256)
            spread = jnp.dot(both, expand[:, lanes], preferred_element_type=F32)
            part = ops[start : start + CHUNK, lanes].astype(F32)
            weighted = part * spread[:CHUNK]
            pulled = part * spread[CHUNK:]
            column = column + (pulled[:, :128] + pulled[:, 128:])
            wide[pl.ds(2 * t, CHUNK, stride=tiles), :] = weighted[:, :128]
            wide[pl.ds(2 * t + 1, CHUNK, stride=tiles), :] = weighted[:, 128:]
        folded[...] = column + pltpu.roll(column, points, 1)
        if k >= 2:
            store(k - 2).wait()
        slot = built.at[k % 2]
        column = jnp.where(
            low_half,
            folded[pl.ds(0, CHUNK // 2, stride=2), :],
            folded[pl.ds(1, CHUNK // 2, stride=2), :],
        )
        high, middle, low = [piece.astype(F32)[:, None, :] for piece in split3(column)]
        extra = jnp.where(extra_row == 2, low, 0.0)
        extra = jnp.where(extra_row == 1, middle, extra)
        slot[:, 128:144, :] = jnp.where(extra_row == 0, high, extra).astype(BF16)

        def pair_up(step, carried, slot=slot):
            for i in range(CHUNK // 2):
                pair = step * (CHUNK // 2) + i
                place = pl.multiple_of(pair * 2 * tiles, 2 * tiles)
                first = wide[pl.ds(place, tiles), :]
                second = wide[pl.ds(place + tiles, tiles), :]
                pieces = [
                    jnp.where(low_half, first, 0.0),
                    jnp.where(low_half, pltpu.roll(first, points, 1), 0.0),
                    jnp.where(low_half, 0.0, pltpu.roll(second, points, 1)),
                    jnp.where(low_half, 0.0, second),
                ]
                for q in range(4):
                    slot[pair, q * tiles : (q + 1) * tiles, :] = pieces[q].astype(BF16)
            return carried

        lax.fori_loop(0, 1, pair_up, 0)
        store(k).start()
        reads[k].wait()
        if k >= 2:
            store_own(k - 2).wait()
        turned[k % 2] = jnp.swapaxes(levels[:, k * some : (k + 1) * some, :], 0, 1)
        store_own(k).start()
    store_own(steps - 2).wait()
    store_own(steps - 1).wait()
    store(steps - 2).wait()
    store(steps - 1).wait()


def prepare(obs_count, obs_op, rinv_blocks, innov_blocks, anomalies):
    blocks, width = obs_op.shape
    lev_dev, col_dev, members = anomalies.shape
    steps = blocks // CHUNK
    vmem = pl.BlockSpec(memory_space=pltpu.VMEM)
    anywhere = pl.BlockSpec(memory_space=pl.ANY)
    return pl.pallas_call(
        prepare_kernel,
        in_specs=[pl.BlockSpec(memory_space=pltpu.SMEM), anywhere, vmem, vmem, anywhere],
        out_specs=[anywhere, vmem, anywhere],
        out_shape=[
            jax.ShapeDtypeStruct((blocks // 2, 144, 128), BF16),
            jax.ShapeDtypeStruct((8, 256), F32),
            jax.ShapeDtypeStruct((col_dev, lev_dev, members), BF16),
        ],
        scratch_shapes=[
            pltpu.VMEM((blocks, width), BF16),
            pltpu.VMEM(anomalies.shape, BF16),
            pltpu.VMEM((128, width), BF16),
            pltpu.VMEM((CHUNK * width // 128, 128), F32),
            pltpu.VMEM((CHUNK, 128), F32),
            pltpu.VMEM((2, CHUNK // 2, 144, 128), BF16),
            pltpu.VMEM((2, col_dev // steps, lev_dev, members), BF16),
            pltpu.SemaphoreType.DMA((steps,)),
            pltpu.SemaphoreType.DMA((steps,)),
            pltpu.SemaphoreType.DMA((2,)),
            pltpu.SemaphoreType.DMA((2,)),
        ],
        compiler_params=pltpu.CompilerParams(vmem_limit_bytes=52 << 20),
        name="prepare_operators",
    )(obs_count, obs_op, rinv_blocks, innov_blocks, anomalies)


def gram_kernel(
    cols_ref, count_ref, core_ref, own_ref, remote_ref, pair_ref, sums_ref,
    keep_ref, give_ref, table, pairs, support_a, support_b, scaled_a, scaled_b, total, pulled, sems,
):
    own_cols = own_ref.shape[0]
    group_pairs = GROUP // 2
    own = pltpu.make_async_copy(own_ref, table.at[pl.ds(0, own_cols)], sems.at[2])
    remote = pltpu.make_async_copy(
        remote_ref, table.at[pl.ds(own_cols, remote_ref.shape[0])], sems.at[3]
    )
    own.start()
    remote.start()
    groups = (count_ref[0] + GROUP - 1) // GROUP

    def fetch(g):
        part = pl.ds(g * group_pairs, group_pairs)
        return pltpu.make_async_copy(pair_ref.at[part], pairs.at[g % 2], sems.at[g % 2])

    fetch(0).start()
    total[...] = jnp.zeros_like(total)
    pulled[...] = jnp.zeros_like(pulled)
    remote.wait()
    own.wait()

    half = GROUP // 2
    most_halves = cols_ref.shape[0] // (half * 8)

    def collect(h, support):
        place = jnp.minimum(h, most_halves - 1) * (half * 8)
        for i in range(half * 8):
            support[i] = table[cols_ref[place + i]]

    def add(operators, first, support, scaled):
        extra = jnp.zeros((16, 256), F32)
        for j in range(half // 2):
            points = support[j * 16 : (j + 1) * 16].reshape(128, 256)
            images = jnp.dot(operators[first + j], points, preferred_element_type=F32)
            scaled[j * 128 : (j + 1) * 128, :] = images[:128].astype(BF16)
            extra = extra + images[128:]
        pulled[...] += extra
        rows = scaled[...]
        total[...] += lax.dot_general(
            rows, rows, (((0,), (0,)), ((), ())), preferred_element_type=F32
        )

    def step(g, carried):
        fetch(g).wait()

        @pl.when(g + 1 < groups)
        def _():
            fetch(g + 1).start()

        operators = pairs.at[g % 2]
        collect(2 * g + 1, support_b)
        add(operators, 0, support_a, scaled_a)
        collect(2 * g + 2, support_a)
        add(operators, half // 2, support_b, scaled_b)
        return carried

    collect(0, support_a)
    lax.fori_loop(0, groups, step, 0)

    projection = pulled[0:1, :] + pulled[1:2, :] + pulled[2:3, :]
    rows = lax.broadcasted_iota(jnp.int32, (128, 128), 0)
    lanes = lax.broadcasted_iota(jnp.int32, (128, 128), 1)
    corner = total[128:256, 128:256]
    left = jnp.where(lanes >= rows, total[0:128, 0:128], corner)
    diagonal = jnp.sum(jnp.where(lanes == rows, corner, 0.0), axis=0, keepdims=True)
    diagonal = jnp.concatenate([diagonal, jnp.zeros((1, 128), F32)], axis=1)
    row = lax.broadcasted_iota(jnp.int32, (16, 256), 0)
    sums = jnp.concatenate([sums_ref[...], sums_ref[...]], axis=0)
    ending = jnp.where(row == 2, sums, 0.0)
    ending = jnp.where(row == 1, diagonal, ending)
    ending = jnp.where(row == 0, projection, ending)
    packed = jnp.concatenate([left, total[0:128, 128:256]], axis=1)
    first = packed[0:PACK]
    second = jnp.concatenate([packed[PACK:128], ending], axis=0)
    core = core_ref[0]

    @pl.when(core == 0)
    def _():
        keep_ref[...] = first
        give_ref[...] = second

    @pl.when(core != 0)
    def _():
        keep_ref[...] = second
        give_ref[...] = first


def gram_sums(obs_cols, obs_count, core, own, remote, pairs, sums):
    vmem = pl.BlockSpec(memory_space=pltpu.VMEM)
    smem = pl.BlockSpec(memory_space=pltpu.SMEM)
    anywhere = pl.BlockSpec(memory_space=pl.ANY)
    half = jax.ShapeDtypeStruct((PACK, 256), F32)
    return pl.pallas_call(
        gram_kernel,
        in_specs=[smem, smem, smem, anywhere, anywhere, anywhere, vmem],
        out_specs=[vmem, vmem],
        out_shape=[half, half],
        scratch_shapes=[
            pltpu.VMEM((own.shape[0] + remote.shape[0],) + own.shape[1:], BF16),
            pltpu.VMEM((2, GROUP // 2) + pairs.shape[1:], BF16),
            pltpu.VMEM((GROUP * 4, 8, 256), BF16),
            pltpu.VMEM((GROUP * 4, 8, 256), BF16),
            pltpu.VMEM((GROUP * 32, 256), BF16),
            pltpu.VMEM((GROUP * 32, 256), BF16),
            pltpu.VMEM((256, 256), F32),
            pltpu.VMEM((16, 256), F32),
            pltpu.SemaphoreType.DMA((4,)),
        ],
        compiler_params=pltpu.CompilerParams(vmem_limit_bytes=50 << 20),
        name="gram_sums",
    )(obs_cols, obs_count, core, own, remote, pairs, sums)


def dot3(left, right):
    left_high = left.astype(BF16)
    left_low = (left - left_high.astype(F32)).astype(BF16)
    right_high = right.astype(BF16)
    right_low = (right - right_high.astype(F32)).astype(BF16)
    return jnp.dot(
        jnp.concatenate([left_high, left_high, left_low], axis=1),
        jnp.concatenate([right_high, right_low, right_high], axis=0),
        preferred_element_type=F32,
    )


def apply_kernel(
    core_ref, mine_ref, other_ref, mean_ref, anom_ref, out_ref,
    levels, results, means, approx_ref, inverse_ref, in_sems, out_sems,
):
    lev_dev = anom_ref.shape[0]
    members = anom_ref.shape[2]
    loads = [
        pltpu.make_async_copy(anom_ref.at[v], levels.at[v], in_sems.at[v]) for v in range(lev_dev)
    ]
    for load in loads:
        load.start()
    core = core_ref[0]
    mine, other = mine_ref[...], other_ref[...]
    packed = jnp.concatenate(
        [jnp.where(core == 0, mine, other), jnp.where(core == 0, other, mine)], axis=0
    )
    half_rows = lax.broadcasted_iota(jnp.int32, (128, 128), 0)
    half_lanes = lax.broadcasted_iota(jnp.int32, (128, 128), 1)
    left, right = packed[0:128, 0:128], packed[0:128, 128:256]
    turned = left.T
    first = jnp.where(half_lanes >= half_rows, left, turned)
    last = jnp.where(half_lanes > half_rows, turned, left)
    last = jnp.where(half_lanes == half_rows, packed[129:130, 0:128], last)
    gram = jnp.concatenate(
        [
            jnp.concatenate([first, right], axis=1),
            jnp.concatenate([right.T, last], axis=1),
        ],
        axis=0,
    )
    projection = packed[128:129]
    sums = packed[130:131]
    rows = lax.broadcasted_iota(jnp.int32, (members, members), 0)
    lanes = lax.broadcasted_iota(jnp.int32, (members, members), 1)
    means[...] = mean_ref[...].T

    numerator, obs_total = sums[:, 0:1], sums[:, 1:2]
    shift = (members - 1.0) * obs_total / numerator
    identity = jnp.where(rows == lanes, 1.0, 0.0)
    system = gram + shift * identity
    norm = jnp.sqrt(jnp.sum(system * system, axis=(0, 1), keepdims=True))
    lowest = jnp.minimum(jnp.sqrt(shift / norm), 1.0)[0, 0]

    def factor(scale, product):
        return (1.5 * scale) * identity - (0.5 * scale * scale * scale) * product

    def next_scale(low):
        x = jnp.maximum(low, 0.02)
        scale = 1.7323 + x * (-0.88804 + x * (-0.071549 + x * (0.385863 - 0.15965 * x)))
        scale = jnp.maximum(scale, 1.0)
        at_low = 0.5 * scale * low * (3.0 - scale * scale * low * low)
        at_one = 0.5 * scale * (3.0 - scale * scale)
        return scale, jnp.minimum(at_low, at_one)

    def more(carried):
        turn, low = carried
        return jnp.logical_and(turn < 60, low < 0.999)

    def advance(carried):
        turn, low = carried
        scale, low = next_scale(low)
        approx, inverse = approx_ref[...], inverse_ref[...]
        middle = factor(scale, dot3(inverse, approx))
        approx_ref[...] = dot3(approx, middle)
        inverse_ref[...] = dot3(middle, inverse)
        return turn + 1, low

    start = system / norm
    scale, lowest = next_scale(lowest)
    middle = factor(scale, start)
    approx_ref[...] = dot3(start, middle)
    inverse_ref[...] = middle
    lax.while_loop(more, advance, (jnp.int32(0), lowest))
    inverse = inverse_ref[...]
    inverse = dot3(factor(1.0, dot3(inverse, approx_ref[...])), inverse)
    line = jnp.broadcast_to(projection, (128, members)).T
    weights = dot3(inverse, dot3(inverse, line)) / norm
    root = (jnp.sqrt((members - 1.0) / norm)) * inverse
    transform = (root + jnp.concatenate([weights, weights], axis=1)).astype(BF16)

    stores = []
    for v in range(lev_dev):
        loads[v].wait()
        updated = jnp.dot(levels[v], transform, preferred_element_type=F32)
        results[v] = (means[:, v : v + 1] + updated).astype(BF16)
        stores.append(pltpu.make_async_copy(results.at[v], out_ref.at[v], out_sems.at[v]))
        stores[v].start()
    for store in stores:
        store.wait()


def solve_and_apply(core, mine, other, mean_state, anomalies):
    vmem = pl.BlockSpec(memory_space=pltpu.VMEM)
    anywhere = pl.BlockSpec(memory_space=pl.ANY)
    lev_dev, col_dev, members = anomalies.shape
    return pl.pallas_call(
        apply_kernel,
        in_specs=[pl.BlockSpec(memory_space=pltpu.SMEM), vmem, vmem, vmem, anywhere],
        out_specs=anywhere,
        out_shape=jax.ShapeDtypeStruct(anomalies.shape, BF16),
        scratch_shapes=[
            pltpu.VMEM(anomalies.shape, BF16),
            pltpu.VMEM(anomalies.shape, BF16),
            pltpu.VMEM((col_dev, lev_dev), F32),
            pltpu.VMEM((members, members), F32),
            pltpu.VMEM((members, members), F32),
            pltpu.SemaphoreType.DMA((lev_dev,)),
            pltpu.SemaphoreType.DMA((lev_dev,)),
        ],
        compiler_params=pltpu.CompilerParams(vmem_limit_bytes=53 << 20),
        name="solve_and_apply",
    )(core, mine, other, mean_state, anomalies)


def swap(value, devices, mask):
    return lax.ppermute(value, AXES, [(d, d ^ mask) for d in range(devices)])


def sum_over(value, devices, one, two):
    arrived = [swap(value, devices, mask) for mask in (one, two, one | two)]
    return (value + arrived[0]) + (arrived[1] + arrived[2])


def per_device(
    devices, anomalies, mean_state, obs_op, innovations, obs_rinv, obs_cols, send_cols, obs_count
):
    blocks = obs_op.shape[0]
    per_block = innovations.shape[0] // blocks
    core = (lax.axis_index("lev") % 2).astype(jnp.int32).reshape(1)
    outgoing = gather_sent(send_cols, anomalies)
    remote = lax.all_to_all(outgoing, "tile", split_axis=0, concat_axis=0, tiled=True)

    rinv_blocks = obs_rinv.reshape(blocks, per_block)
    innov_blocks = innovations.reshape(blocks, per_block)
    pairs, sums, own = prepare(obs_count, obs_op, rinv_blocks, innov_blocks, anomalies)
    keep, give = gram_sums(obs_cols, obs_count, core, own, remote, pairs, sums)
    value = keep + swap(give, devices, 1)
    for one, two in ((2, 8), (32, 6), (24, 96)):
        value = sum_over(value, devices, one, two)
    other = swap(value, devices, 1)
    return solve_and_apply(core, value, other, mean_state, anomalies)


def solution(mesh):
    return jax.shard_map(
        functools.partial(per_device, mesh.size),
        mesh=mesh,
        in_specs=(
            P("lev", "tile", None),
            P("lev", "tile"),
            P(("tile", "lev"), None),
            P(("tile", "lev")),
            P(("tile", "lev")),
            P(("tile", "lev")),
            P("tile", None),
            P(("tile", "lev")),
        ),
        out_specs=P("lev", "tile", None),
        check_vma=False,
    )
```

```python
import functools

import jax
import jax.numpy as jnp
from jax import lax
from jax.experimental import pallas as pl
from jax.experimental.pallas import tpu as pltpu
from jax.sharding import PartitionSpec as P

F32 = jnp.float32
BF16 = jnp.bfloat16
AXES = ("tile", "lev")
GROUP = 128
CHUNK = 64
PACK = 72


def split3(value):
    high = value.astype(BF16)
    rest = value - high.astype(F32)
    middle = rest.astype(BF16)
    low = (rest - middle.astype(F32)).astype(BF16)
    return high, middle, low


def send_kernel(send_ref, anom_ref, out_ref, levels, table, picked, sems, out_sems):
    col_dev = anom_ref.shape[1]
    slots = out_ref.shape[0]
    steps = sems.shape[0]
    some = col_dev // steps
    copies = []
    for k in range(steps):
        part = pl.ds(k * some, some)
        copies.append(pltpu.make_async_copy(anom_ref.at[:, part], levels.at[:, part], sems.at[k]))
        copies[k].start()
    for k in range(steps):
        copies[k].wait()
        part = slice(k * some, (k + 1) * some)
        table[part] = jnp.swapaxes(levels[:, part, :], 0, 1)

    batch = slots // 6
    stores = []
    for k in range(6):
        for i in range(batch):
            slot = k * batch + i
            picked[slot] = table[send_ref[0, slot]]
        part = pl.ds(k * batch, batch)
        stores.append(pltpu.make_async_copy(picked.at[part], out_ref.at[part], out_sems.at[k]))
        stores[k].start()
    for store in stores:
        store.wait()


def gather_sent(send_cols, anomalies):
    lev_dev, col_dev, members = anomalies.shape
    slots = send_cols.shape[1]
    return pl.pallas_call(
        send_kernel,
        in_specs=[pl.BlockSpec(memory_space=pltpu.SMEM), pl.BlockSpec(memory_space=pl.ANY)],
        out_specs=pl.BlockSpec(memory_space=pl.ANY),
        out_shape=jax.ShapeDtypeStruct((slots, lev_dev, members), BF16),
        scratch_shapes=[
            pltpu.VMEM((lev_dev, col_dev, members), BF16),
            pltpu.VMEM((col_dev, lev_dev, members), BF16),
            pltpu.VMEM((slots, lev_dev, members), BF16),
            pltpu.SemaphoreType.DMA((8,)),
            pltpu.SemaphoreType.DMA((6,)),
        ],
        compiler_params=pltpu.CompilerParams(vmem_limit_bytes=60 << 20),
        name="gather_sent",
    )(send_cols, anomalies)


def prepare_kernel(
    count_ref, op_ref, rinv_ref, innov_ref, anom_ref, pair_ref, sums_ref, own_ref,
    ops, levels, expand, wide, folded, built, turned, in_sems, anom_sems, out_sems, own_sems,
):
    blocks, width = op_ref.shape
    per_block = rinv_ref.shape[1]
    points = width // per_block
    tiles = width // 128
    count = count_ref[0]
    steps = blocks // CHUNK
    loads = []
    for k in range(steps):
        part = pl.ds(k * CHUNK, CHUNK)
        loads.append(pltpu.make_async_copy(op_ref.at[part], ops.at[part], in_sems.at[k]))
        loads[k].start()
    col_dev = anom_ref.shape[1]
    some = col_dev // steps
    reads = []
    for k in range(steps):
        part = pl.ds(k * some, some)
        reads.append(
            pltpu.make_async_copy(anom_ref.at[:, part], levels.at[:, part], anom_sems.at[k])
        )
        reads[k].start()
    spread_row = lax.broadcasted_iota(jnp.int32, (2 * per_block, 256), 0)
    spread_row = jnp.where(spread_row < per_block, spread_row, spread_row - per_block) * points
    ahead = lax.broadcasted_iota(jnp.int32, (2 * per_block, 256), 1) - spread_row
    for t in range(tiles // 2):
        inside = jnp.logical_and(ahead >= -t * 256, ahead < points - t * 256)
        expand[:, t * 256 : (t + 1) * 256] = jnp.where(inside, 1.0, 0.0).astype(BF16)
    live = lax.broadcasted_iota(jnp.int32, (blocks, per_block), 0) < count
    innov = innov_ref[...]
    squares = jnp.where(live, rinv_ref[...] * innov * innov, 0.0)
    numerator = jnp.sum(squares, axis=(0, 1), keepdims=True)
    total = jnp.full((1, 1), count * per_block, jnp.int32).astype(F32)
    lane = lax.broadcasted_iota(jnp.int32, (8, 256), 1)
    sums_ref[...] = jnp.where(lane == 0, numerator, jnp.where(lane == 1, total, 0.0))
    low_half = lax.broadcasted_iota(jnp.int32, (1, 128), 1) < points
    extra_row = lax.broadcasted_iota(jnp.int32, (CHUNK // 2, 16, 128), 1)

    def store(k):
        part = pl.ds(k * (CHUNK // 2), CHUNK // 2)
        return pltpu.make_async_copy(built.at[k % 2], pair_ref.at[part], out_sems.at[k % 2])

    def store_own(k):
        part = pl.ds(k * some, some)
        return pltpu.make_async_copy(turned.at[k % 2], own_ref.at[part], own_sems.at[k % 2])

    for k in range(steps):
        start = k * CHUNK
        alive = start + lax.broadcasted_iota(jnp.int32, (CHUNK, per_block), 0) < count
        rinv = jnp.where(alive, rinv_ref[start : start + CHUNK, :], 0.0)
        factors = jnp.concatenate([jnp.sqrt(rinv), rinv * innov_ref[start : start + CHUNK, :]], 0)
        high, middle, _ = split3(factors)
        both = jnp.concatenate([high, middle], axis=1)
        loads[k].wait()
        column = jnp.zeros((CHUNK, 128), F32)
        for t in range(tiles // 2):
            lanes = slice(t * 256, (t + 1) * 256)
            spread = jnp.dot(both, expand[:, lanes], preferred_element_type=F32)
            part = ops[start : start + CHUNK, lanes].astype(F32)
            weighted = part * spread[:CHUNK]
            pulled = part * spread[CHUNK:]
            column = column + (pulled[:, :128] + pulled[:, 128:])
            wide[pl.ds(2 * t, CHUNK, stride=tiles), :] = weighted[:, :128]
            wide[pl.ds(2 * t + 1, CHUNK, stride=tiles), :] = weighted[:, 128:]
        folded[...] = column + pltpu.roll(column, points, 1)
        if k >= 2:
            store(k - 2).wait()
        slot = built.at[k % 2]
        column = jnp.where(
            low_half,
            folded[pl.ds(0, CHUNK // 2, stride=2), :],
            folded[pl.ds(1, CHUNK // 2, stride=2), :],
        )
        high, middle, low = [piece.astype(F32)[:, None, :] for piece in split3(column)]
        extra = jnp.where(extra_row == 2, low, 0.0)
        extra = jnp.where(extra_row == 1, middle, extra)
        slot[:, 128:144, :] = jnp.where(extra_row == 0, high, extra).astype(BF16)

        def pair_up(step, carried, slot=slot):
            for i in range(CHUNK // 2):
                pair = step * (CHUNK // 2) + i
                place = pl.multiple_of(pair * 2 * tiles, 2 * tiles)
                first = wide[pl.ds(place, tiles), :]
                second = wide[pl.ds(place + tiles, tiles), :]
                pieces = [
                    jnp.where(low_half, first, 0.0),
                    jnp.where(low_half, pltpu.roll(first, points, 1), 0.0),
                    jnp.where(low_half, 0.0, pltpu.roll(second, points, 1)),
                    jnp.where(low_half, 0.0, second),
                ]
                for q in range(4):
                    slot[pair, q * tiles : (q + 1) * tiles, :] = pieces[q].astype(BF16)
            return carried

        lax.fori_loop(0, 1, pair_up, 0)
        store(k).start()
        reads[k].wait()
        if k >= 2:
            store_own(k - 2).wait()
        turned[k % 2] = jnp.swapaxes(levels[:, k * some : (k + 1) * some, :], 0, 1)
        store_own(k).start()
    store_own(steps - 2).wait()
    store_own(steps - 1).wait()
    store(steps - 2).wait()
    store(steps - 1).wait()


def prepare(obs_count, obs_op, rinv_blocks, innov_blocks, anomalies):
    blocks, width = obs_op.shape
    lev_dev, col_dev, members = anomalies.shape
    steps = blocks // CHUNK
    vmem = pl.BlockSpec(memory_space=pltpu.VMEM)
    anywhere = pl.BlockSpec(memory_space=pl.ANY)
    return pl.pallas_call(
        prepare_kernel,
        in_specs=[pl.BlockSpec(memory_space=pltpu.SMEM), anywhere, vmem, vmem, anywhere],
        out_specs=[anywhere, vmem, anywhere],
        out_shape=[
            jax.ShapeDtypeStruct((blocks // 2, 144, 128), BF16),
            jax.ShapeDtypeStruct((8, 256), F32),
            jax.ShapeDtypeStruct((col_dev, lev_dev, members), BF16),
        ],
        scratch_shapes=[
            pltpu.VMEM((blocks, width), BF16),
            pltpu.VMEM(anomalies.shape, BF16),
            pltpu.VMEM((128, width), BF16),
            pltpu.VMEM((CHUNK * width // 128, 128), F32),
            pltpu.VMEM((CHUNK, 128), F32),
            pltpu.VMEM((2, CHUNK // 2, 144, 128), BF16),
            pltpu.VMEM((2, col_dev // steps, lev_dev, members), BF16),
            pltpu.SemaphoreType.DMA((steps,)),
            pltpu.SemaphoreType.DMA((steps,)),
            pltpu.SemaphoreType.DMA((2,)),
            pltpu.SemaphoreType.DMA((2,)),
        ],
        compiler_params=pltpu.CompilerParams(vmem_limit_bytes=52 << 20),
        name="prepare_operators",
    )(obs_count, obs_op, rinv_blocks, innov_blocks, anomalies)


def gram_kernel(
    cols_ref, count_ref, core_ref, own_ref, remote_ref, pair_ref, sums_ref,
    keep_ref, give_ref, table, pairs, support_a, support_b, scaled_a, scaled_b, total, pulled, sems,
):
    own_cols = own_ref.shape[0]
    group_pairs = GROUP // 2
    own = pltpu.make_async_copy(own_ref, table.at[pl.ds(0, own_cols)], sems.at[2])
    remote = pltpu.make_async_copy(
        remote_ref, table.at[pl.ds(own_cols, remote_ref.shape[0])], sems.at[3]
    )
    own.start()
    remote.start()
    groups = (count_ref[0] + GROUP - 1) // GROUP

    def fetch(g):
        part = pl.ds(g * group_pairs, group_pairs)
        return pltpu.make_async_copy(pair_ref.at[part], pairs.at[g % 2], sems.at[g % 2])

    fetch(0).start()
    total[...] = jnp.zeros_like(total)
    pulled[...] = jnp.zeros_like(pulled)
    remote.wait()
    own.wait()

    half = GROUP // 2
    most_halves = cols_ref.shape[0] // (half * 8)

    def collect(h, support):
        place = jnp.minimum(h, most_halves - 1) * (half * 8)
        for i in range(half * 8):
            support[i] = table[cols_ref[place + i]]

    def add(operators, first, support, scaled):
        extra = jnp.zeros((16, 256), F32)
        for j in range(half // 2):
            points = support[j * 16 : (j + 1) * 16].reshape(128, 256)
            images = jnp.dot(operators[first + j], points, preferred_element_type=F32)
            scaled[j * 128 : (j + 1) * 128, :] = images[:128].astype(BF16)
            extra = extra + images[128:]
        pulled[...] += extra
        rows = scaled[...]
        total[...] += lax.dot_general(
            rows, rows, (((0,), (0,)), ((), ())), preferred_element_type=F32
        )

    def step(g, carried):
        fetch(g).wait()

        @pl.when(g + 1 < groups)
        def _():
            fetch(g + 1).start()

        operators = pairs.at[g % 2]
        collect(2 * g + 1, support_b)
        add(operators, 0, support_a, scaled_a)
        collect(2 * g + 2, support_a)
        add(operators, half // 2, support_b, scaled_b)
        return carried

    collect(0, support_a)
    lax.fori_loop(0, groups, step, 0)

    projection = pulled[0:1, :] + pulled[1:2, :] + pulled[2:3, :]
    rows = lax.broadcasted_iota(jnp.int32, (128, 128), 0)
    lanes = lax.broadcasted_iota(jnp.int32, (128, 128), 1)
    corner = total[128:256, 128:256]
    left = jnp.where(lanes >= rows, total[0:128, 0:128], corner)
    diagonal = jnp.sum(jnp.where(lanes == rows, corner, 0.0), axis=0, keepdims=True)
    diagonal = jnp.concatenate([diagonal, jnp.zeros((1, 128), F32)], axis=1)
    row = lax.broadcasted_iota(jnp.int32, (16, 256), 0)
    sums = jnp.concatenate([sums_ref[...], sums_ref[...]], axis=0)
    ending = jnp.where(row == 2, sums, 0.0)
    ending = jnp.where(row == 1, diagonal, ending)
    ending = jnp.where(row == 0, projection, ending)
    packed = jnp.concatenate([left, total[0:128, 128:256]], axis=1)
    first = packed[0:PACK]
    second = jnp.concatenate([packed[PACK:128], ending], axis=0)
    core = core_ref[0]

    @pl.when(core == 0)
    def _():
        keep_ref[...] = first
        give_ref[...] = second

    @pl.when(core != 0)
    def _():
        keep_ref[...] = second
        give_ref[...] = first


def gram_sums(obs_cols, obs_count, core, own, remote, pairs, sums):
    vmem = pl.BlockSpec(memory_space=pltpu.VMEM)
    smem = pl.BlockSpec(memory_space=pltpu.SMEM)
    anywhere = pl.BlockSpec(memory_space=pl.ANY)
    half = jax.ShapeDtypeStruct((PACK, 256), F32)
    return pl.pallas_call(
        gram_kernel,
        in_specs=[smem, smem, smem, anywhere, anywhere, anywhere, vmem],
        out_specs=[vmem, vmem],
        out_shape=[half, half],
        scratch_shapes=[
            pltpu.VMEM((own.shape[0] + remote.shape[0],) + own.shape[1:], BF16),
            pltpu.VMEM((2, GROUP // 2) + pairs.shape[1:], BF16),
            pltpu.VMEM((GROUP * 4, 8, 256), BF16),
            pltpu.VMEM((GROUP * 4, 8, 256), BF16),
            pltpu.VMEM((GROUP * 32, 256), BF16),
            pltpu.VMEM((GROUP * 32, 256), BF16),
            pltpu.VMEM((256, 256), F32),
            pltpu.VMEM((16, 256), F32),
            pltpu.SemaphoreType.DMA((4,)),
        ],
        compiler_params=pltpu.CompilerParams(vmem_limit_bytes=50 << 20),
        name="gram_sums",
    )(obs_cols, obs_count, core, own, remote, pairs, sums)


def dot3(left, right):
    left_high = left.astype(BF16)
    left_low = (left - left_high.astype(F32)).astype(BF16)
    right_high = right.astype(BF16)
    right_low = (right - right_high.astype(F32)).astype(BF16)
    return jnp.dot(
        jnp.concatenate([left_high, left_high, left_low], axis=1),
        jnp.concatenate([right_high, right_low, right_high], axis=0),
        preferred_element_type=F32,
    )


def apply_kernel(
    core_ref, mine_ref, other_ref, mean_ref, anom_ref, out_ref,
    levels, results, means, approx_ref, inverse_ref, in_sems, out_sems,
):
    lev_dev = anom_ref.shape[0]
    members = anom_ref.shape[2]
    loads = [
        pltpu.make_async_copy(anom_ref.at[v], levels.at[v], in_sems.at[v]) for v in range(lev_dev)
    ]
    for load in loads:
        load.start()
    core = core_ref[0]
    mine, other = mine_ref[...], other_ref[...]
    packed = jnp.concatenate(
        [jnp.where(core == 0, mine, other), jnp.where(core == 0, other, mine)], axis=0
    )
    half_rows = lax.broadcasted_iota(jnp.int32, (128, 128), 0)
    half_lanes = lax.broadcasted_iota(jnp.int32, (128, 128), 1)
    left, right = packed[0:128, 0:128], packed[0:128, 128:256]
    turned = left.T
    first = jnp.where(half_lanes >= half_rows, left, turned)
    last = jnp.where(half_lanes > half_rows, turned, left)
    last = jnp.where(half_lanes == half_rows, packed[129:130, 0:128], last)
    gram = jnp.concatenate(
        [
            jnp.concatenate([first, right], axis=1),
            jnp.concatenate([right.T, last], axis=1),
        ],
        axis=0,
    )
    projection = packed[128:129]
    sums = packed[130:131]
    rows = lax.broadcasted_iota(jnp.int32, (members, members), 0)
    lanes = lax.broadcasted_iota(jnp.int32, (members, members), 1)
    means[...] = mean_ref[...].T

    numerator, obs_total = sums[:, 0:1], sums[:, 1:2]
    shift = (members - 1.0) * obs_total / numerator
    identity = jnp.where(rows == lanes, 1.0, 0.0)
    system = gram + shift * identity
    norm = jnp.sqrt(jnp.sum(system * system, axis=(0, 1), keepdims=True))
    lowest = jnp.minimum(jnp.sqrt(shift / norm), 1.0)[0, 0]

    def factor(scale, product):
        return (1.5 * scale) * identity - (0.5 * scale * scale * scale) * product

    def next_scale(low):
        x = jnp.maximum(low, 0.02)
        scale = 1.7323 + x * (-0.88804 + x * (-0.071549 + x * (0.385863 - 0.15965 * x)))
        scale = jnp.maximum(scale, 1.0)
        at_low = 0.5 * scale * low * (3.0 - scale * scale * low * low)
        at_one = 0.5 * scale * (3.0 - scale * scale)
        return scale, jnp.minimum(at_low, at_one)

    def more(carried):
        turn, low = carried
        return jnp.logical_and(turn < 60, low < 0.999)

    def advance(carried):
        turn, low = carried
        scale, low = next_scale(low)
        approx, inverse = approx_ref[...], inverse_ref[...]
        middle = factor(scale, dot3(inverse, approx))
        approx_ref[...] = dot3(approx, middle)
        inverse_ref[...] = dot3(middle, inverse)
        return turn + 1, low

    start = system / norm
    scale, lowest = next_scale(lowest)
    middle = factor(scale, start)
    approx_ref[...] = dot3(start, middle)
    inverse_ref[...] = middle
    lax.while_loop(more, advance, (jnp.int32(0), lowest))
    inverse = inverse_ref[...]
    inverse = dot3(factor(1.0, dot3(inverse, approx_ref[...])), inverse)
    line = jnp.broadcast_to(projection, (128, members)).T
    weights = dot3(inverse, dot3(inverse, line)) / norm
    root = (jnp.sqrt((members - 1.0) / norm)) * inverse
    transform = (root + jnp.concatenate([weights, weights], axis=1)).astype(BF16)

    stores = []
    some = anom_ref.shape[1] // 2
    for v in range(lev_dev):
        loads[v].wait()
        for h in range(2):
            part = slice(h * some, (h + 1) * some)
            updated = jnp.dot(levels[v, part], transform, preferred_element_type=F32)
            results[v, part] = (means[part, v : v + 1] + updated).astype(BF16)
            place = pl.ds(h * some, some)
            stores.append(
                pltpu.make_async_copy(
                    results.at[v, place], out_ref.at[v, place], out_sems.at[2 * v + h]
                )
            )
            stores[-1].start()
    for store in stores:
        store.wait()


def solve_and_apply(core, mine, other, mean_state, anomalies):
    vmem = pl.BlockSpec(memory_space=pltpu.VMEM)
    anywhere = pl.BlockSpec(memory_space=pl.ANY)
    lev_dev, col_dev, members = anomalies.shape
    return pl.pallas_call(
        apply_kernel,
        in_specs=[pl.BlockSpec(memory_space=pltpu.SMEM), vmem, vmem, vmem, anywhere],
        out_specs=anywhere,
        out_shape=jax.ShapeDtypeStruct(anomalies.shape, BF16),
        scratch_shapes=[
            pltpu.VMEM(anomalies.shape, BF16),
            pltpu.VMEM(anomalies.shape, BF16),
            pltpu.VMEM((col_dev, lev_dev), F32),
            pltpu.VMEM((members, members), F32),
            pltpu.VMEM((members, members), F32),
            pltpu.SemaphoreType.DMA((lev_dev,)),
            pltpu.SemaphoreType.DMA((2 * lev_dev,)),
        ],
        compiler_params=pltpu.CompilerParams(vmem_limit_bytes=53 << 20),
        name="solve_and_apply",
    )(core, mine, other, mean_state, anomalies)


def swap(value, devices, mask):
    return lax.ppermute(value, AXES, [(d, d ^ mask) for d in range(devices)])


def sum_over(value, devices, one, two):
    arrived = [swap(value, devices, mask) for mask in (one, two, one | two)]
    return (value + arrived[0]) + (arrived[1] + arrived[2])


def per_device(
    devices, anomalies, mean_state, obs_op, innovations, obs_rinv, obs_cols, send_cols, obs_count
):
    blocks = obs_op.shape[0]
    per_block = innovations.shape[0] // blocks
    core = (lax.axis_index("lev") % 2).astype(jnp.int32).reshape(1)
    outgoing = gather_sent(send_cols, anomalies)
    remote = lax.all_to_all(outgoing, "tile", split_axis=0, concat_axis=0, tiled=True)

    rinv_blocks = obs_rinv.reshape(blocks, per_block)
    innov_blocks = innovations.reshape(blocks, per_block)
    pairs, sums, own = prepare(obs_count, obs_op, rinv_blocks, innov_blocks, anomalies)
    keep, give = gram_sums(obs_cols, obs_count, core, own, remote, pairs, sums)
    value = keep + swap(give, devices, 1)
    for one, two in ((2, 8), (32, 6), (24, 96)):
        value = sum_over(value, devices, one, two)
    other = swap(value, devices, 1)
    return solve_and_apply(core, value, other, mean_state, anomalies)


def solution(mesh):
    return jax.shard_map(
        functools.partial(per_device, mesh.size),
        mesh=mesh,
        in_specs=(
            P("lev", "tile", None),
            P("lev", "tile"),
            P(("tile", "lev"), None),
            P(("tile", "lev")),
            P(("tile", "lev")),
            P(("tile", "lev")),
            P("tile", None),
            P(("tile", "lev")),
        ),
        out_specs=P("lev", "tile", None),
        check_vma=False,
    )
```
